512 devices in a mesh: sec: 2 (over y_hi), grp: 64 (over y_lo, z, core), tp: 4 (over x).
Axes of the slice: x: 4, y: 8 (y_hi: 2, y_lo: 4; y = y_hi * 4 + y_lo), z: 8, core: 2. Of those that a mesh axis runs over, the one named last changes fastest.
Arguments:
- residual: bfloat16 [256, 6144], P(('sec', 'grp'), 'tp'), may hold values from -30 to 30
- queries: bfloat16 [256, 6144], P(('sec', 'grp'), 'tp'), may hold values from -16 to 16
- key_pages: bfloat16 [3072, 16, 1024], P(('sec', 'grp'), None, 'tp'), may hold values from -32 to 32
- value_pages: bfloat16 [3072, 16, 1024], P(('sec', 'grp'), None, 'tp'), may hold values from -6 to 6
- page_table: int32 [128, 24], P(('sec', 'grp')), may hold values from 0 to 23, each once within a row
- lengths: int32 [128, 2], P(('sec', 'grp')), may hold values from 1 to 192, 288 in all within a row
- norm_gain: bfloat16 [6144], P('tp'), may hold values from 0.099609375 to 1.8984375
- expert_ids: int32 [256, 4], P(('sec', 'grp')), may hold values from 0 to 7, all different within a row; in each aligned block of 2 rows (0 to 1, 2 to 3, ...) at most 2 rows name the same one
- route_gates: float32 [256, 4], P(('sec', 'grp')), may hold values from 0.1 to 1
- w_gate: bfloat16 [6144, 43008], P('tp', ('sec', 'grp')), may hold values from -0.078125 to 0.078125
- w_up: bfloat16 [6144, 43008], P('tp', ('sec', 'grp')), may hold values from -0.078125 to 0.078125
- w_down: bfloat16 [43008, 6144], P(('sec', 'grp'), 'tp'), may hold values from -0.078125 to 0.078125
Outputs:
- layer_out: bfloat16 [256, 6144], P(('sec', 'grp'), 'tp')
The draws below stay inside these ranges and needn't reach their ends.
Inputs may be any that keep to these rules, and one draw needn't show every extreme that they name: `page_table`: each row lists every local page once; sequence i uses entries i * 12 to i * 12 + 11 in order. The 2 lengths of one row sum to 288; each is at most 192. `expert_ids`: each row names 4 different experts; in each aligned block of 2 rows (the rows of one device) no expert is named by more than 2 rows, and some block names some expert exactly 2 times.
All inputs are finite; a program needn't handle non-finite values.
Results may differ from the reference program's by a relative error of at most 0.0053.
Values may be sent and summed in bfloat16 or wider, within the bound.
A program may use at most 64 MiB of HBM per device.

```python
import math
import jax
import jax.numpy as jnp
import numpy as np
from jax import lax

D = 6144
HEADS = 48
KV_HEADS = 8
HEAD_DIM = 128
EXPERTS = 8
FF = 5376
TOPK = 4
PAGE = 16
PMAX = 12
SEQ_DEV = 2
CAP = 2
PAGES_DEV = 24
LTOT = 288
ROWS = 256
NPAGES = 3072
N_SEC = 2
N_GRP = 64


def draw_residual(key, part):
    key = jax.random.fold_in(key, 13)
    column = jnp.arange(D, dtype=jnp.float32)[None, :]
    factor = 0.5 * (1.0 + 2.0 * column / D)
    values = jnp.clip(jax.random.normal(key, (ROWS, D), jnp.float32), -6.0, 6.0) * factor
    return values.astype(jnp.bfloat16)


def draw_queries(key, part):
    key = jax.random.fold_in(key, 11)
    base = jnp.clip(jax.random.normal(key, (ROWS, D), jnp.float32), -6.0, 6.0)
    return base.astype(jnp.bfloat16)


def draw_key_pages(key, part):
    key = jax.random.fold_in(key, 12)
    base = jnp.clip(jax.random.normal(key, (NPAGES, PAGE, KV_HEADS * HEAD_DIM), jnp.float32), -6.0, 6.0)
    return base.astype(jnp.bfloat16)


def block_levels(own_key, dims, split, smallest, high):
    gain, own = 1.0, jax.random.fold_in(own_key, 6)
    for axis_at, blocks in split:
        steps = jnp.exp(jax.random.uniform(jax.random.fold_in(own, axis_at), (blocks,), jnp.float32, smallest / len(split), high / len(split)))
        gain = gain * jnp.repeat(steps, dims[axis_at] // blocks).reshape([-1 if axis == axis_at else 1 for axis in range(len(dims))])
    return gain


def split_up(count, total, reach, slope):
    portions = [(1 << 20) // math.isqrt(grade ** slope) + 1 for grade in range(2, count + 1)]
    spare, given = total - reach - (count - 1), [1] * (count - 1)
    while spare > 0:
        movable = [i for i in range(count - 1) if given[i] < reach]
        pool, remaining = sum([portions[i] for i in movable]), spare
        for i in movable:
            extra = min(reach - given[i], max(1, remaining * portions[i] // pool), spare)
            given[i] = given[i] + extra
            spare = spare - extra
    return np.array([reach] + given)


def ragged_sizes(stream_key, number_of, total, limit, slope):
    if number_of == 2:
        one = jax.random.randint(stream_key, (), max(1, total - limit), min(limit, total - 1) + 1)
        return jnp.stack([one, total - one])
    tallies = jnp.asarray(split_up(number_of, total, limit, slope), jnp.int32)
    pairs = (number_of - 1) // 2
    donor, sink = tallies[1:1 + 2 * pairs:2], tallies[2:2 + 2 * pairs:2]
    slack = jnp.minimum(donor - 1, limit - sink)
    shifted = jax.random.randint(jax.random.fold_in(stream_key, 1), (pairs,), 0, 1 << 20) % (slack + 1)
    tallies = tallies.at[1:1 + 2 * pairs:2].set(donor - shifted).at[2:2 + 2 * pairs:2].set(sink + shifted)
    return tallies[jax.random.permutation(jax.random.fold_in(stream_key, 2), number_of)]


def deal_out(own_key, own, number, rows, count, top, most, slope):
    ranking = jax.random.permutation(own_key, count)
    heavy_load, ordinary = shares(count, rows * top, most, slope, True), shares(count, rows * top, most, slope, False)
    places = jnp.arange(count)

    def named(tallies, rotation):
        used = int((tallies > 0).sum())
        fixed = max(1, used // 4)
        moved = fixed + (places - fixed + rotation * (used - fixed)) % max(1, count - fixed)
        return jnp.zeros((count,), jnp.int32).at[ranking[jnp.where(places < fixed, places, moved)]].set(jnp.asarray(tallies, jnp.int32))

    tallies = jnp.where(number % 4 == 0, named(heavy_load, number // 4), named(ordinary, number - number // 4 - 1))
    mixed = jax.random.permutation(jax.random.fold_in(own, 3), count)
    source_of, taker = mixed[0:count // 2 * 2:2], mixed[1:count // 2 * 2:2]
    room = jnp.minimum(tallies[source_of] - 1, most - tallies[taker]) // 2
    room = jnp.where((source_of == ranking[0]) | (taker == ranking[0]) | (tallies[taker] == 0), 0, jnp.maximum(room, 0))
    moved = jax.random.randint(jax.random.fold_in(own, 4), (count // 2,), 0, 1 << 20) % (room + 1)
    tallies = tallies.at[source_of].add(-moved).at[taker].add(moved)
    items = jnp.searchsorted(jnp.cumsum(tallies), jnp.arange(rows * top), side="right").astype(jnp.int32)
    table = items.reshape(top, rows).T
    table = table[jax.random.permutation(jax.random.fold_in(own, 1), rows)]
    rotation = jax.random.randint(jax.random.fold_in(own, 2), (rows, 1), 0, top)
    return jnp.take_along_axis(table, (jnp.arange(top)[None, :] + rotation) % top, axis=1)


def shares(count, total, reach, lean, full):
    portions = [(1 << 20) // math.isqrt(grade ** lean) + 1 for grade in range(1, count + 1)]
    largest = reach if full else min(reach, max(-(-total // count), total * portions[0] // sum(portions)))
    least = 1 if total - largest >= count - 1 else 0
    holding, surplus = [largest] + [least] * (count - 1), total - largest - least * (count - 1)
    while surplus > 0:
        movable = [i for i in range(1, count) if holding[i] < largest] or [i for i in range(1, count) if holding[i] < reach]
        mass, left = sum([portions[i] for i in movable]), surplus
        for i in movable:
            addition = min(reach - holding[i], max(1, left * portions[i] // mass), surplus)
            holding[i] = holding[i] + addition
            surplus = surplus - addition
    return np.array(holding)


def bell_draw(key, dims, width, bound, pieces=(), kind=jnp.bfloat16):
    result = jax.random.normal(key, dims, jnp.float32) * width
    if len(pieces) > 0:
        result = block_levels(key, dims, pieces, -0.22, 0.18) * result
    return jnp.clip(result, min=-bound, max=bound).astype(kind)


def setup_inputs(seed: int = 0) -> dict:
    seeds = jax.random.split(jax.random.key(seed), 13)
    residual = draw_residual(jax.random.fold_in(seeds[12], 71), 0)
    queries = draw_queries(jax.random.fold_in(seeds[12], 71), 0)
    key_pages = draw_key_pages(jax.random.fold_in(seeds[12], 71), 0)
    value_pages = bell_draw(seeds[3], (NPAGES, PAGE, KV_HEADS * HEAD_DIM), 1.0, 6.0, ((0, 128), (2, 4)))
    page_table = jax.vmap(lambda own: jax.random.permutation(own, PAGES_DEV))(jax.random.split(seeds[4], (N_SEC * N_GRP))).reshape((N_SEC * N_GRP, PAGES_DEV)).astype(jnp.int32)
    lengths = jax.vmap(lambda own: ragged_sizes(own, SEQ_DEV, LTOT, PMAX * PAGE, 2))(jax.random.split(seeds[5], (N_SEC * N_GRP))).reshape((N_SEC * N_GRP, SEQ_DEV)).astype(jnp.int32)
    norm_gain = jnp.clip(1.0 + 0.18 * jax.random.normal(seeds[6], (D,), jnp.float32), 0.099609375, 1.8984375).astype(jnp.bfloat16)
    expert_ids_keys = jax.random.split(jax.random.fold_in(seeds[7], 1), ROWS // SEQ_DEV)
    expert_ids_turns = jax.random.permutation(jax.random.fold_in(seeds[7], 3), ROWS // SEQ_DEV)
    expert_ids = jax.vmap(lambda own, number: deal_out(jax.random.fold_in(seeds[7], 2), own, number, SEQ_DEV, EXPERTS, TOPK, CAP, 2))(expert_ids_keys, expert_ids_turns).reshape((ROWS, TOPK))
    route_gates = jnp.clip(jnp.exp(math.log(1.0) - 2.3025851 * jax.random.uniform(seeds[8], (ROWS, TOPK), jnp.float32) ** block_levels(seeds[8], (ROWS, TOPK), ((0, 128),), -0.2, 0.2)), 0.1, 1.0)
    w_gate = bell_draw(seeds[9], (D, EXPERTS * FF), D ** -0.5, 0.078125, ((0, 4), (1, 128)))
    w_up = bell_draw(seeds[10], (D, EXPERTS * FF), D ** -0.5, 0.078125, ((0, 4), (1, 128)))
    w_down = bell_draw(seeds[11], (EXPERTS * FF, D), FF ** -0.5, 0.078125, ((0, 128), (1, 4)))
    return dict(residual=residual, queries=queries, key_pages=key_pages, value_pages=value_pages, page_table=page_table, lengths=lengths, norm_gain=norm_gain, expert_ids=expert_ids, route_gates=route_gates, w_gate=w_gate, w_up=w_up, w_down=w_down)


def attend_group(args):
    group_keys, group_values, page_rows, group_queries, group_lengths = args
    key_span = PMAX * PAGE
    key_rows = group_keys[page_rows].reshape(SEQ_DEV, key_span, KV_HEADS, HEAD_DIM).astype(jnp.float32)
    value_rows = group_values[page_rows].reshape(SEQ_DEV, key_span, KV_HEADS, HEAD_DIM).astype(jnp.float32)
    query_heads = group_queries.reshape(SEQ_DEV, KV_HEADS, HEADS // KV_HEADS, HEAD_DIM).astype(jnp.float32)
    scores = jnp.einsum('sagh,slah->sagl', query_heads, key_rows) * HEAD_DIM ** (-0.5)
    visible = jnp.arange(key_span, dtype=jnp.int32)[None, :] < group_lengths[:, None]
    scores = jnp.where(visible[:, None, None, :], scores, jnp.float32(-1e+30))
    top_score = lax.optimization_barrier(jnp.max(scores, axis=-1, keepdims=True))
    expo = jnp.exp(scores - top_score)
    attn_probs = (expo / lax.optimization_barrier(jnp.sum(expo, axis=-1, keepdims=True))).astype(jnp.bfloat16)
    attn_out = jnp.einsum('sagl,slah->sagh', attn_probs.astype(jnp.float32), value_rows)
    return attn_out.reshape(SEQ_DEV, D)

def reference(residual, queries, key_pages, value_pages, page_table, lengths, norm_gain, expert_ids, route_gates, w_gate, w_up, w_down):
    groups = N_SEC * N_GRP
    page_keys = key_pages.reshape(groups, PAGES_DEV, PAGE, KV_HEADS * HEAD_DIM)
    page_values = value_pages.reshape(groups, PAGES_DEV, PAGE, KV_HEADS * HEAD_DIM)
    page_rows = page_table.reshape(groups, SEQ_DEV, PMAX)
    grouped_queries = queries.reshape(groups, SEQ_DEV, D)
    attn_out = lax.map(attend_group, (page_keys, page_values, page_rows, grouped_queries, lengths))
    attn_out = attn_out.reshape(ROWS, D)
    stream = (residual.astype(jnp.float32) + attn_out).astype(jnp.bfloat16)
    stream_f32 = stream.astype(jnp.float32)
    mean_square = lax.optimization_barrier(jnp.mean(stream_f32 * stream_f32, axis=1, keepdims=True))
    normed = (stream_f32 * lax.rsqrt(mean_square + 1e-05) * norm_gain.astype(jnp.float32)).astype(jnp.bfloat16)
    route_weight = route_gates / lax.optimization_barrier(jnp.sum(route_gates, axis=1, keepdims=True))
    matches = (expert_ids[:, :, None] == jnp.arange(EXPERTS, dtype=jnp.int32)[None, None, :]).astype(jnp.float32)
    expert_weight = lax.optimization_barrier(jnp.sum(matches * route_weight[:, :, None], axis=1))

    def one_expert(total, index):
        start = (index * FF).astype(jnp.int32)
        gate_cols = lax.dynamic_slice_in_dim(w_gate, start, FF, 1)
        up_cols = lax.dynamic_slice_in_dim(w_up, start, FF, 1)
        down_rows = lax.dynamic_slice_in_dim(w_down, start, FF, 0)
        gate_proj = jnp.dot(normed, gate_cols, preferred_element_type=jnp.float32)
        up_proj = jnp.dot(normed, up_cols, preferred_element_type=jnp.float32)
        hidden = (jax.nn.silu(gate_proj) * up_proj).astype(jnp.bfloat16)
        expert_out = jnp.dot(hidden, down_rows, preferred_element_type=jnp.float32)
        column = lax.dynamic_index_in_dim(expert_weight, index, 1, keepdims=True)
        return (total + column * expert_out, None)
    total, unused = lax.scan(one_expert, jnp.zeros((ROWS, D), jnp.float32), jnp.arange(EXPERTS, dtype=jnp.int32))
    return (stream_f32 + total).astype(jnp.bfloat16)
```

```python
import functools

import jax
import jax.numpy as jnp
from jax import lax
from jax.experimental import pallas as pl
from jax.experimental.pallas import tpu as pltpu
from jax.sharding import PartitionSpec as P

MESH = pl.DeviceIdType.MESH
BF16, F32 = jnp.bfloat16, jnp.float32

D = 6144
RING = 8
NX = 4
HEADS_DEV = 12
HD = 128
COLS = 1536
EXT = COLS + HD
FFD = 336
FFP = 384
PAGES = 24
PAGE = 16
KV = PAGES * PAGE
BLK = 32
SS_HI, SS_LO = FFD % HD, FFD % HD + 1

CHUNKS = ((0, 1), (7, 2), (6, 3), (5, 4))
NC = len(CHUNKS)
PLACE = {m: (j, i) for j, pair in enumerate(CHUNKS) for i, m in enumerate(pair)}


def kernel(
    res_hbm, q_hbm, k_hbm, v_hbm, gain_hbm, wg_hbm, wu_hbm, wd_hbm,
    pt, lens, ids, gates,
    out_ref,
    res, q, kp, vp, gain, wg, wu, wd,
    s24, blk, p1, f16, xall, pay, rsb, hid, csend, crecv, r1s, r1r, r2s, r2r,
    ld_sem, p1_s, p1_r, p2_s, p2_r, fw_s, fw_r, rs_s, rs_r, ag_s, ag_r,
    co_s, co_r, r1_s, r1_r, r2_sm, r2_rm,
):
    sec, grp, x = lax.axis_index("sec"), lax.axis_index("grp"), lax.axis_index("tp")
    y, z, c = sec * 4 + grp // 16, (grp // 2) % 8, grp % 2

    def dev(yy, zz, cc, xx):
        return (yy // 4, (yy % 4) * 16 + zz * 2 + cc, xx)

    def first(k):
        return dev((y + k * (1 - c)) % RING, (z + k * c) % RING, c, x)

    def second(k):
        return dev((y + k * c) % RING, (z + k * (1 - c)) % RING, c, x)

    def along(e):
        return dev(y, z, c, (x + e) % NX)

    other = dev(y, z, 1 - c, x)

    loads = []
    for i, (a, b) in enumerate((
        (q_hbm, q), (k_hbm, kp), (v_hbm, vp), (res_hbm, res), (gain_hbm, gain),
        (wg_hbm, wg), (wu_hbm, wu), (wd_hbm, wd.at[pl.ds(0, FFD)]),
    )):
        cp = pltpu.make_async_copy(a, b, ld_sem.at[i])
        cp.start()
        loads.append(cp)

    barrier = pltpu.get_barrier_semaphore()
    peers = [first(k) for k in range(1, RING)] + [second(k) for k in range(1, RING)]
    peers += [along(e) for e in range(1, NX)] + [other]
    for peer in peers:
        pl.semaphore_signal(barrier, inc=1, device_id=peer, device_id_type=MESH)

    pending = []

    def send(src, dst, ssem, rsem, to):
        cp = pltpu.make_async_remote_copy(
            src_ref=src, dst_ref=dst, send_sem=ssem, recv_sem=rsem,
            device_id=to, device_id_type=MESH,
        )
        cp.start()
        pending.append(cp)
        return cp

    lane = lax.broadcasted_iota(jnp.int32, (24, KV), 1)
    row = lax.broadcasted_iota(jnp.int32, (24, KV), 0)
    page = lane // PAGE
    slot = jnp.zeros((24, KV), jnp.int32)
    for j in range(PAGES):
        slot = jnp.where(page == pt[0, j], j, slot)
    late = slot >= PAGES // 2
    pos = (slot - jnp.where(late, PAGES // 2, 0)) * PAGE + lane % PAGE
    visible = (pos < jnp.where(late, lens[0, 1], lens[0, 0])) & (
        jnp.where(late, 1, 0) == row % 2
    )
    lane8 = lax.broadcasted_iota(jnp.int32, (8, HD), 1)
    row8 = lax.broadcasted_iota(jnp.int32, (8, HD), 0)
    weight = jnp.zeros((8, HD), F32)
    total = jnp.ones((8, HD), F32)
    for s in range(2):
        here = row8 == s
        total = jnp.where(
            here, gates[s, 0] + gates[s, 1] + gates[s, 2] + gates[s, 3], total
        )
        for k in range(4):
            hit = here & (lane8 < 16) & (lane8 % 8 == ids[s, k])
            weight = jnp.where(hit, gates[s, k], weight)
    weight = weight / total

    wd[FFD:, :] = jnp.zeros((FFP - FFD, COLS), BF16)

    def stack(value):
        for h in range(HEADS_DEV):
            s24[2 * h : 2 * h + 2, :] = value[:, h * HD : (h + 1) * HD]
        return s24[...]

    nt = (((1,), (1,)), ((), ()))
    loads[0].wait()
    q24 = stack(q[...].astype(F32)).astype(BF16)
    loads[1].wait()
    keys = kp[...].reshape(KV, 2 * HD)
    head0 = row < 12
    scores = jnp.where(
        head0,
        lax.dot_general(q24, keys[:, :HD], nt, preferred_element_type=F32),
        lax.dot_general(q24, keys[:, HD:], nt, preferred_element_type=F32),
    ) * (HD ** -0.5)
    scores = jnp.where(visible, scores, F32(-1e30))
    expo = jnp.exp(scores - jnp.max(scores, axis=1, keepdims=True))
    probs = (expo / jnp.sum(expo, axis=1, keepdims=True)).astype(BF16)
    loads[2].wait()
    values = vp[...].reshape(KV, 2 * HD)
    attn = jnp.dot(probs, values, preferred_element_type=F32)
    row24 = lax.broadcasted_iota(jnp.int32, (24, HD), 0)
    attn = jnp.where(row24 < 12, attn[:, :HD], attn[:, HD:])
    loads[3].wait()
    stream = (stack(res[...].astype(F32)) + attn).astype(BF16).astype(F32)
    loads[4].wait()
    gain24 = stack(jnp.broadcast_to(gain[...].astype(F32), (2, COLS)))
    square = jnp.sum(stream * stream, axis=1, keepdims=True)
    odd = lax.broadcasted_iota(jnp.int32, (24, 1), 0) % 2 == 1
    ss0 = jnp.sum(jnp.where(odd, 0.0, square), axis=0, keepdims=True)
    ss1 = jnp.sum(jnp.where(odd, square, 0.0), axis=0, keepdims=True)
    ss = jnp.where(row8 == 0, ss0, ss1)
    w_hi = weight.astype(BF16).astype(F32)
    ss_hi = ss.astype(BF16).astype(F32)
    extra = jnp.where(lane8 < 8, w_hi, jnp.where(lane8 < 16, weight - w_hi, 0.0))
    extra = jnp.where(lane8 == SS_HI, ss_hi, extra)
    extra = jnp.where(lane8 == SS_LO, ss - ss_hi, extra)
    extra = jnp.where(row8 < 2, extra, 0.0)
    blk[...] = jnp.concatenate([stream * gain24, extra], axis=0).astype(BF16)

    pl.semaphore_wait(barrier, len(peers))

    arrive1 = [
        send(blk, p1.at[k], p1_s.at[k], p1_r.at[k], first(k)) for k in range(1, RING)
    ]

    def place(k, value):
        for t in range(EXT // HD):
            f16[2 * k : 2 * k + 2, t * HD : (t + 1) * HD] = value[2 * t : 2 * t + 2, :]

    place(0, blk[...].astype(F32))
    for k in (1, 7, 2, 6, 3, 5, 4):
        arrive1[k - 1].wait_recv()
        place(k, p1[k].astype(F32))
    xall[0, 0:16, :] = f16[...].astype(BF16)

    arrive2 = [None] * RING
    for m in (4, 5, 3, 6, 2, 7, 1):
        j, i = PLACE[m]
        arrive2[m] = send(
            xall.at[0, pl.ds(0, 16)], xall.at[j, pl.ds(16 * i, 16)],
            p2_s.at[m], p2_r.at[m], second(m),
        )
    loads[5].wait()
    loads[6].wait()
    loads[7].wait()

    rs, ag, core, back = {}, {}, {}, {}

    def gate_up(j):
        for m in CHUNKS[j]:
            if m:
                arrive2[m].wait_recv()
        fw = send(
            xall.at[j, pl.ds(0, 32)], xall.at[j, pl.ds(32, 32)],
            fw_s.at[j], fw_r.at[j], other,
        )
        fw.wait_recv()
        rows = xall[j, :, 0:COLS]
        pay[j, :, :, 256:FFP] = xall[j, :, COLS:EXT].reshape(NX, 16, HD)
        pay[j, :, :, 640:768] = jnp.zeros((NX, 16, HD), BF16)
        pay[j, :, :, 0:FFD] = (
            jnp.dot(rows, wg[...], preferred_element_type=F32).astype(BF16).reshape(NX, 16, FFD)
        )
        pay[j, :, :, FFP : FFP + FFD] = (
            jnp.dot(rows, wu[...], preferred_element_type=F32).astype(BF16).reshape(NX, 16, FFD)
        )
        rs[j] = [
            send(
                pay.at[j, (x + e) % NX], rsb.at[j, e],
                rs_s.at[j, e], rs_r.at[j, e], along(e),
            )
            for e in range(1, NX)
        ]

    lane16 = lax.broadcasted_iota(jnp.int32, (16, FFP), 1)
    tile16 = lax.broadcasted_iota(jnp.int32, (16, HD), 1)

    def activate(j):
        both = pay[j, x].astype(F32)
        for e in range(1, NX):
            rs[j][e - 1].wait_recv()
            both = both + rsb[j, e].astype(F32)
        tile = both[:, 256:FFP]
        square = jnp.sum(
            jnp.where((tile16 == SS_HI) | (tile16 == SS_LO), tile, 0.0),
            axis=1, keepdims=True,
        )
        scale = lax.rsqrt(square / D + 1e-05)
        gate = both[:, 0:FFP] * scale
        up = both[:, FFP:] * scale
        value = gate / (1.0 + jnp.exp(-gate)) * up
        hid[j, x] = jnp.where(lane16 < FFD, value, 0.0).astype(BF16)
        ag[j] = [
            send(hid.at[j, x], hid.at[j, x], ag_s.at[j, e], ag_r.at[j, e], along(e))
            for e in range(1, NX)
        ]

    lane64 = lax.broadcasted_iota(jnp.int32, (64, HD), 1)

    def down(j):
        for e in range(1, NX):
            ag[j][e - 1].wait_recv()
        extras = xall[j, :, COLS:EXT].astype(F32)
        weight = jnp.sum(
            jnp.where((lane64 == y) | (lane64 == y + 8), extras, 0.0),
            axis=1, keepdims=True,
        )
        part = jnp.dot(
            hid[j].reshape(64, FFP), wd[...], preferred_element_type=F32
        ) * weight
        csend[j] = part[32:, :].astype(BF16)
        core[j] = send(csend.at[j], crecv.at[j], co_s.at[j], co_r.at[j], other)
        r1s[j] = part[:32, :].astype(BF16)

    def give_back(j):
        core[j].wait_recv()
        r1s[j] = (r1s[j].astype(F32) + crecv[j].astype(F32)).astype(BF16)
        for i, m in enumerate(CHUNKS[j]):
            if m:
                back[m] = send(
                    r1s.at[j, pl.ds(16 * i, 16)], r1r.at[m],
                    r1_s.at[m], r1_r.at[m], second(RING - m),
                )

    for step in range(NC + 3):
        if step < NC:
            gate_up(step)
        if 0 <= step - 1 < NC:
            activate(step - 1)
        if 0 <= step - 2 < NC:
            down(step - 2)
        if 0 <= step - 3 < NC:
            give_back(step - 3)

    f16[:, 0:COLS] = r1s[0, 0:16, :].astype(F32)
    for m in (1, 7, 2, 6, 3, 5, 4):
        back[m].wait_recv()
        f16[:, 0:COLS] += r1r[m].astype(F32)

    home = []
    for k in range(RING):
        for h in range(HEADS_DEV):
            s24[2 * h : 2 * h + 2, :] = f16[2 * k : 2 * k + 2, h * HD : (h + 1) * HD]
        if k == 0:
            mixture = s24[...]
        else:
            r2s[k, 0:24, :] = s24[...].astype(BF16)
            r2s[k, 24:32, :] = jnp.zeros((8, HD), BF16)
            home.append(
                send(r2s.at[k], r2r.at[k], r2_sm.at[k], r2_rm.at[k], first(RING - k))
            )
    for k in (1, 7, 2, 6, 3, 5, 4):
        home[k - 1].wait_recv()
        mixture = mixture + r2r[k, 0:24, :].astype(F32)
    out_ref[...] = (stream + mixture).astype(BF16)
    for cp in pending:
        cp.wait_send()


def shards(
    residual, queries, key_pages, value_pages, page_table, lengths, norm_gain,
    expert_ids, route_gates, w_gate, w_up, w_down,
):
    any_, smem = pl.BlockSpec(memory_space=pl.ANY), pl.BlockSpec(memory_space=pltpu.SMEM)
    dma = pltpu.SemaphoreType.DMA
    out = pl.pallas_call(
        kernel,
        out_shape=jax.ShapeDtypeStruct((24, HD), BF16),
        in_specs=[any_] * 8 + [smem] * 4,
        out_specs=pl.BlockSpec(memory_space=pltpu.VMEM),
        scratch_shapes=[
            pltpu.VMEM((2, COLS), BF16), pltpu.VMEM((2, COLS), BF16),
            pltpu.VMEM((PAGES, PAGE, 2 * HD), BF16), pltpu.VMEM((PAGES, PAGE, 2 * HD), BF16),
            pltpu.VMEM((1, COLS), BF16),
            pltpu.VMEM((COLS, FFD), BF16), pltpu.VMEM((COLS, FFD), BF16),
            pltpu.VMEM((FFP, COLS), BF16),
            pltpu.VMEM((24, HD), F32), pltpu.VMEM((BLK, HD), BF16),
            pltpu.VMEM((RING, BLK, HD), BF16), pltpu.VMEM((16, EXT), F32),
            pltpu.VMEM((NC, 64, EXT), BF16), pltpu.VMEM((NC, NX, 16, 2 * FFP), BF16),
            pltpu.VMEM((NC, NX, 16, 2 * FFP), BF16), pltpu.VMEM((NC, NX, 16, FFP), BF16),
            pltpu.VMEM((NC, 32, COLS), BF16), pltpu.VMEM((NC, 32, COLS), BF16),
            pltpu.VMEM((NC, 32, COLS), BF16), pltpu.VMEM((RING, 16, COLS), BF16),
            pltpu.VMEM((RING, BLK, HD), BF16), pltpu.VMEM((RING, BLK, HD), BF16),
            dma((8,)), dma((RING,)), dma((RING,)), dma((RING,)), dma((RING,)),
            dma((NC,)), dma((NC,)), dma((NC, NX)), dma((NC, NX)), dma((NC, NX)), dma((NC, NX)),
            dma((NC,)), dma((NC,)), dma((RING,)), dma((RING,)), dma((RING,)), dma((RING,)),
        ],
        compiler_params=pltpu.CompilerParams(
            collective_id=0, has_side_effects=True, vmem_limit_bytes=48 * 2**20
        ),
        name="decode_layer",
    )(
        residual, queries, key_pages, value_pages, norm_gain.reshape(1, COLS),
        w_gate, w_up, w_down, page_table, lengths, expert_ids, route_gates,
    )
    return out.reshape(HEADS_DEV, 2, HD).transpose(1, 0, 2).reshape(2, COLS)


def solution(mesh):
    rows, wide = ("sec", "grp"), "tp"
    return jax.shard_map(
        shards,
        mesh=mesh,
        in_specs=(
            P(rows, wide), P(rows, wide), P(rows, None, wide), P(rows, None, wide),
            P(rows, None), P(rows, None), P(wide), P(rows, None), P(rows, None),
            P(wide, rows), P(wide, rows), P(rows, wide),
        ),
        out_specs=P(rows, wide),
        check_vma=False,
    )
```

```python
import functools

import jax
import jax.numpy as jnp
from jax import lax
from jax.experimental import pallas as pl
from jax.experimental.pallas import tpu as pltpu
from jax.sharding import PartitionSpec as P

MESH = pl.DeviceIdType.MESH
BF16, F32 = jnp.bfloat16, jnp.float32

D = 6144
RING = 8
NX = 4
HEADS_DEV = 12
HD = 128
COLS = 1536
EXT = COLS + HD
FFD = 336
FFP = 384
PAGES = 24
PAGE = 16
KV = PAGES * PAGE
BLK = 32
SS_HI, SS_LO = FFD % HD, FFD % HD + 1

CHUNKS = ((4, 5, 3, 6), (7, 2, 1, 0))
STEPS = "F0 G0 F1 G1 A0 A1 D0 E0 D1 E1"
NC = len(CHUNKS)
BASE = [sum(len(c) for c in CHUNKS[:j]) for j in range(NC)]
ROW = {m: 32 * BASE[j] + 16 * i for j, c in enumerate(CHUNKS) for i, m in enumerate(c)}
HALF = {m: 16 * (BASE[j] + i) for j, c in enumerate(CHUNKS) for i, m in enumerate(c)}
FAR = (4, 5, 3, 6, 2, 7, 1)
NEAR = FAR[::-1]


def kernel(
    res_hbm, q_hbm, k_hbm, v_hbm, gain_hbm, wg_hbm, wu_hbm, wd_hbm,
    pt_hbm, lens_hbm, ids_hbm, gates_hbm,
    out_ref,
    pt, lens, ids, gates, res, q, kp, vp, gain, wgu, wd,
    s24, blk, p1, f16, xall, pay, rsb, hid, csend, crecv, r1s, r1r, r2s, r2r,
    ld_sem, p1_s, p1_r, p2_s, p2_r, fw_s, fw_r, rs_s, rs_r, ag_s, ag_r,
    co_s, co_r, r1_s, r1_r, r2_sm, r2_rm,
):
    sec, grp, x = lax.axis_index("sec"), lax.axis_index("grp"), lax.axis_index("tp")
    y, z, c = sec * 4 + grp // 16, (grp // 2) % 8, grp % 2

    def dev(yy, zz, cc, xx):
        return (yy // 4, (yy % 4) * 16 + zz * 2 + cc, xx)

    def first(k):
        return dev((y + k * (1 - c)) % RING, (z + k * c) % RING, c, x)

    def second(k):
        return dev((y + k * c) % RING, (z + k * (1 - c)) % RING, c, x)

    def along(e):
        return dev(y, z, c, (x + e) % NX)

    other = dev(y, z, 1 - c, x)

    barrier = pltpu.get_barrier_semaphore()
    peers = [ring(k) for k in FAR for ring in (first, second)]
    peers += [along(e) for e in range(1, NX)] + [other]
    for peer in peers:
        pl.semaphore_signal(barrier, inc=1, device_id=peer, device_id_type=MESH)

    loads = []
    for i, (a, b) in enumerate((
        (pt_hbm, pt), (lens_hbm, lens), (ids_hbm, ids), (gates_hbm, gates),
        (q_hbm, q), (k_hbm, kp), (v_hbm, vp), (res_hbm, res), (gain_hbm, gain),
        (wg_hbm, wgu.at[pl.ds(0, FFD)]), (wu_hbm, wgu.at[pl.ds(FFP, FFD)]),
        (wd_hbm, wd.at[pl.ds(0, FFD)]),
    )):
        cp = pltpu.make_async_copy(a, b, ld_sem.at[i])
        cp.start()
        loads.append(cp)

    pending = []

    def send(src, dst, ssem, rsem, to):
        cp = pltpu.make_async_remote_copy(
            src_ref=src, dst_ref=dst, send_sem=ssem, recv_sem=rsem,
            device_id=to, device_id_type=MESH,
        )
        cp.start()
        pending.append(cp)
        return cp

    lane = lax.broadcasted_iota(jnp.int32, (8, KV), 1)
    row = lax.broadcasted_iota(jnp.int32, (8, KV), 0)
    page = lane // PAGE
    slot = jnp.zeros((8, KV), jnp.int32)
    loads[0].wait()
    loads[1].wait()
    for j in range(PAGES):
        slot = jnp.where(page == pt[0, j], j, slot)
    late = slot >= PAGES // 2
    pos = (slot - jnp.where(late, PAGES // 2, 0)) * PAGE + lane % PAGE
    visible = (pos < jnp.where(late, lens[0, 1], lens[0, 0])) & (
        jnp.where(late, 1, 0) == row % 2
    )
    hidden_tokens = jnp.where(visible, 0.0, F32(-1e30))
    hidden_tokens = jnp.concatenate([hidden_tokens] * 3, axis=0)
    loads[2].wait()
    loads[3].wait()
    lane8 = lax.broadcasted_iota(jnp.int32, (8, HD), 1)
    row8 = lax.broadcasted_iota(jnp.int32, (8, HD), 0)
    weight = jnp.zeros((8, HD), F32)
    total = jnp.ones((8, HD), F32)
    for s in range(2):
        here = row8 == s
        total = jnp.where(
            here, gates[s, 0] + gates[s, 1] + gates[s, 2] + gates[s, 3], total
        )
        for k in range(4):
            hit = here & (lane8 < 16) & (lane8 % 8 == ids[s, k])
            weight = jnp.where(hit, gates[s, k], weight)
    weight = weight / total

    wd[FFD:, :] = jnp.zeros((FFP - FFD, COLS), BF16)
    wgu[FFD:FFP, :] = jnp.zeros((FFP - FFD, COLS), BF16)
    wgu[FFP + FFD :, :] = jnp.zeros((FFP - FFD, COLS), BF16)

    def stack(value):
        for h in range(HEADS_DEV):
            s24[2 * h : 2 * h + 2, :] = value[:, h * HD : (h + 1) * HD]
        return s24[...]

    nt = (((1,), (1,)), ((), ()))
    loads[4].wait()
    q24 = stack(q[...].astype(F32)).astype(BF16)
    loads[5].wait()
    keys = kp[...].reshape(KV, 2 * HD)
    head0 = lax.broadcasted_iota(jnp.int32, (24, KV), 0) < 12
    scores = jnp.where(
        head0,
        lax.dot_general(q24, keys[:, :HD], nt, preferred_element_type=F32),
        lax.dot_general(q24, keys[:, HD:], nt, preferred_element_type=F32),
    ) * (HD ** -0.5)
    scores = jnp.where(hidden_tokens < 0.0, hidden_tokens, scores)
    expo = jnp.exp(scores - jnp.max(scores, axis=1, keepdims=True))
    probs = (expo / jnp.sum(expo, axis=1, keepdims=True)).astype(BF16)
    loads[6].wait()
    values = vp[...].reshape(KV, 2 * HD)
    attn = jnp.dot(probs, values, preferred_element_type=F32)
    row24 = lax.broadcasted_iota(jnp.int32, (24, HD), 0)
    attn = jnp.where(row24 < 12, attn[:, :HD], attn[:, HD:])
    loads[7].wait()
    stream = (stack(res[...].astype(F32)) + attn).astype(BF16).astype(F32)
    loads[8].wait()
    gains = gain[...].astype(F32).reshape(HEADS_DEV, HD)
    for h in range(HEADS_DEV):
        s24[2 * h : 2 * h + 2, :] = jnp.broadcast_to(gains[h : h + 1, :], (2, HD))
    gain24 = s24[...]
    square = jnp.sum(stream * stream, axis=1, keepdims=True)
    odd = lax.broadcasted_iota(jnp.int32, (24, 1), 0) % 2 == 1
    ss0 = jnp.sum(jnp.where(odd, 0.0, square), axis=0, keepdims=True)
    ss1 = jnp.sum(jnp.where(odd, square, 0.0), axis=0, keepdims=True)
    ss = jnp.where(row8 == 0, ss0, ss1)
    w_hi = weight.astype(BF16).astype(F32)
    ss_hi = ss.astype(BF16).astype(F32)
    extra = jnp.where(lane8 < 8, w_hi, jnp.where(lane8 < 16, weight - w_hi, 0.0))
    extra = jnp.where(lane8 == SS_HI, ss_hi, extra)
    extra = jnp.where(lane8 == SS_LO, ss - ss_hi, extra)
    extra = jnp.where(row8 < 2, extra, 0.0)
    blk[...] = jnp.concatenate([stream * gain24, extra], axis=0).astype(BF16)

    pl.semaphore_wait(barrier, len(peers))

    arrive1 = [
        send(blk, p1.at[k], p1_s.at[k], p1_r.at[k], first(k)) for k in range(1, RING)
    ]

    def place(k, value):
        for t in range(EXT // HD):
            f16[2 * k : 2 * k + 2, t * HD : (t + 1) * HD] = value[2 * t : 2 * t + 2, :]

    place(0, blk[...].astype(F32))
    for k in NEAR:
        arrive1[k - 1].wait_recv()
        place(k, p1[k].astype(F32))
    own = pl.ds(ROW[0], 16)
    xall[own, :] = f16[...].astype(BF16)

    arrive2 = {
        m: send(
            xall.at[own], xall.at[pl.ds(ROW[m], 16)], p2_s.at[m], p2_r.at[m], second(m)
        )
        for m in FAR
    }
    for cp in loads[9:]:
        cp.wait()

    forwards, rs, ag, core, back = {}, {}, {}, {}, {}

    def quarter(j, q):
        size = 8 * len(CHUNKS[j])
        return pl.ds(pl.multiple_of(32 * BASE[j] + q * size, 16), size)

    def forward(j):
        n, base = len(CHUNKS[j]), 32 * BASE[j]
        forwards[j] = []
        for i, m in enumerate(CHUNKS[j]):
            if m:
                arrive2[m].wait_recv()
            forwards[j].append(send(
                xall.at[pl.ds(base + 16 * i, 16)],
                xall.at[pl.ds(base + 16 * (n + i), 16)],
                fw_s.at[m], fw_r.at[m], other,
            ))

    def gate_up(j):
        n, base = len(CHUNKS[j]), 32 * BASE[j]
        for cp in forwards[j]:
            cp.wait_recv()
        rows = pl.ds(base, 32 * n)
        both = lax.dot_general(
            xall[rows, 0:COLS], wgu[...], nt, preferred_element_type=F32
        )
        lane = lax.broadcasted_iota(jnp.int32, (32 * n, HD), 1)
        extras = xall[rows, COLS:EXT].astype(F32)
        tile = jnp.where(lane >= FFD % HD, extras, both[:, 256:FFP])
        pay[rows, 0:256] = both[:, 0:256].astype(BF16)
        pay[rows, 256:FFP] = tile.astype(BF16)
        pay[rows, FFP:] = both[:, FFP:].astype(BF16)
        piece = pl.ds(8 * BASE[j], 8 * n)
        rs[j] = [
            send(
                pay.at[quarter(j, (x + e) % NX)], rsb.at[e, piece],
                rs_s.at[j, e], rs_r.at[j, e], along(e),
            )
            for e in (2, 1, 3)
        ]

    def activate(j):
        n = len(CHUNKS[j])
        both = pay[quarter(j, x), :].astype(F32)
        lane = lax.broadcasted_iota(jnp.int32, (8 * n, HD), 1)
        weight = jnp.sum(
            jnp.where(
                (lane == y) | (lane == y + 8),
                xall[quarter(j, x), COLS:EXT].astype(F32), 0.0,
            ),
            axis=1, keepdims=True,
        )
        for cp, e in zip(rs[j], (2, 1, 3)):
            cp.wait_recv()
            both = both + rsb[e, pl.ds(8 * BASE[j], 8 * n), :].astype(F32)
        square = jnp.sum(
            jnp.where((lane == SS_HI) | (lane == SS_LO), both[:, 256:FFP], 0.0),
            axis=1, keepdims=True,
        )
        scale = lax.rsqrt(square / D + 1e-05)
        gate = both[:, 0:FFP] * scale
        up = both[:, FFP:] * (scale * weight)
        value = gate / (1.0 + jnp.exp(-gate)) * up
        unit = lax.broadcasted_iota(jnp.int32, (8 * n, FFP), 1)
        mine = quarter(j, x)
        hid[mine, :] = jnp.where(unit < FFD, value, 0.0).astype(BF16)
        ag[j] = [
            send(hid.at[mine], hid.at[mine], ag_s.at[j, e], ag_r.at[j, e], along(e))
            for e in (2, 1, 3)
        ]

    def down(j):
        n, base = len(CHUNKS[j]), 32 * BASE[j]
        half = pl.ds(16 * BASE[j], 16 * n)
        for cp in ag[j]:
            cp.wait_recv()
        theirs = pl.ds(base + 16 * n, 16 * n)
        csend[half, :] = jnp.dot(
            hid[theirs, :], wd[...], preferred_element_type=F32
        ).astype(BF16)
        core[j] = send(csend.at[half], crecv.at[half], co_s.at[j], co_r.at[j], other)
        mine = pl.ds(base, 16 * n)
        r1s[half, :] = jnp.dot(
            hid[mine, :], wd[...], preferred_element_type=F32
        ).astype(BF16)

    def give_back(j):
        core[j].wait_recv()
        half = pl.ds(16 * BASE[j], 16 * len(CHUNKS[j]))
        r1s[half, :] = (r1s[half, :].astype(F32) + crecv[half, :].astype(F32)).astype(BF16)
        for m in FAR:
            if m in CHUNKS[j]:
                back[m] = send(
                    r1s.at[pl.ds(HALF[m], 16)], r1r.at[m],
                    r1_s.at[m], r1_r.at[m], second(RING - m),
                )

    stages = {"F": forward, "G": gate_up, "A": activate, "D": down, "E": give_back}
    for step in STEPS.split():
        stages[step[0]](int(step[1:]))

    total = r1s[pl.ds(HALF[0], 16), :].astype(F32)
    for m in NEAR:
        back[m].wait_recv()
        total = total + r1r[m].astype(F32)
    f16[:, 0:COLS] = total

    home = {}
    for k in FAR + (0,):
        for h in range(HEADS_DEV):
            s24[2 * h : 2 * h + 2, :] = f16[2 * k : 2 * k + 2, h * HD : (h + 1) * HD]
        if k:
            r2s[k, 0:24, :] = s24[...].astype(BF16)
            r2s[k, 24:32, :] = jnp.zeros((8, HD), BF16)
            home[k] = send(
                r2s.at[k], r2r.at[k], r2_sm.at[k], r2_rm.at[k], first(RING - k)
            )
    mixture = s24[...]
    for cp in pending[: -len(FAR)]:
        cp.wait_send()
    for k in NEAR:
        home[k].wait_recv()
        mixture = mixture + r2r[k, 0:24, :].astype(F32)
    out_ref[...] = (stream + mixture).astype(BF16)
    for cp in pending[-len(FAR) :]:
        cp.wait_send()


def shards(
    residual, queries, key_pages, value_pages, page_table, lengths, norm_gain,
    expert_ids, route_gates, w_gate, w_up, w_down,
):
    any_ = pl.BlockSpec(memory_space=pl.ANY)
    dma = pltpu.SemaphoreType.DMA
    out = pl.pallas_call(
        kernel,
        out_shape=jax.ShapeDtypeStruct((24, HD), BF16),
        in_specs=[any_] * 12,
        out_specs=pl.BlockSpec(memory_space=pltpu.VMEM),
        scratch_shapes=[
            pltpu.SMEM((1, PAGES), jnp.int32), pltpu.SMEM((1, 2), jnp.int32),
            pltpu.SMEM((2, 4), jnp.int32), pltpu.SMEM((2, 4), F32),
            pltpu.VMEM((2, COLS), BF16), pltpu.VMEM((2, COLS), BF16),
            pltpu.VMEM((PAGES, PAGE, 2 * HD), BF16), pltpu.VMEM((PAGES, PAGE, 2 * HD), BF16),
            pltpu.VMEM((COLS,), BF16),
            pltpu.VMEM((2 * FFP, COLS), BF16),
            pltpu.VMEM((FFP, COLS), BF16),
            pltpu.VMEM((24, HD), F32), pltpu.VMEM((BLK, HD), BF16),
            pltpu.VMEM((RING, BLK, HD), BF16), pltpu.VMEM((16, EXT), F32),
            pltpu.VMEM((256, EXT), BF16), pltpu.VMEM((256, 2 * FFP), BF16),
            pltpu.VMEM((NX, 64, 2 * FFP), BF16), pltpu.VMEM((256, FFP), BF16),
            pltpu.VMEM((128, COLS), BF16), pltpu.VMEM((128, COLS), BF16),
            pltpu.VMEM((128, COLS), BF16), pltpu.VMEM((RING, 16, COLS), BF16),
            pltpu.VMEM((RING, BLK, HD), BF16), pltpu.VMEM((RING, BLK, HD), BF16),
            dma((12,)), dma((RING,)), dma((RING,)), dma((RING,)), dma((RING,)),
            dma((RING,)), dma((RING,)), dma((NC, NX)), dma((NC, NX)), dma((NC, NX)), dma((NC, NX)),
            dma((NC,)), dma((NC,)), dma((RING,)), dma((RING,)), dma((RING,)), dma((RING,)),
        ],
        compiler_params=pltpu.CompilerParams(
            collective_id=0, has_side_effects=True, vmem_limit_bytes=60 * 2**20
        ),
        name="decode_layer",
    )(
        residual, queries, key_pages, value_pages, norm_gain,
        w_gate.T, w_up.T, w_down, page_table, lengths, expert_ids, route_gates,
    )
    return out.reshape(HEADS_DEV, 2, HD).transpose(1, 0, 2).reshape(2, COLS)


def solution(mesh):
    rows, wide = ("sec", "grp"), "tp"
    return jax.shard_map(
        shards,
        mesh=mesh,
        in_specs=(
            P(rows, wide), P(rows, wide), P(rows, None, wide), P(rows, None, wide),
            P(rows, None), P(rows, None), P(wide), P(rows, None), P(rows, None),
            P(wide, rows), P(wide, rows), P(rows, wide),
        ),
        out_specs=P(rows, wide),
        check_vma=False,
    )
```

```python
import functools

import jax
import jax.numpy as jnp
from jax import lax
from jax.experimental import pallas as pl
from jax.experimental.pallas import tpu as pltpu
from jax.sharding import PartitionSpec as P

MESH = pl.DeviceIdType.MESH
BF16, F32 = jnp.bfloat16, jnp.float32

D = 6144
RING = 8
NX = 4
HEADS_DEV = 12
HD = 128
COLS = 1536
EXT = COLS + HD
FFD = 336
FFP = 384
WIDE = 2 * FFP
PAGES = 24
PAGE = 16
KV = PAGES * PAGE
BLK = 32
SS_HI, SS_LO = FFD % HD, FFD % HD + 1

CHUNKS = ((4, 5, 3, 6), (7, 2, 1, 0))
STEPS = ("G0", "G1", "A0", "A1", "D0", "D1")
NC = len(CHUNKS)
BASE = [sum(len(c) for c in CHUNKS[:j]) for j in range(NC)]
ROW = {m: 16 * (BASE[j] + i) for j, c in enumerate(CHUNKS) for i, m in enumerate(c)}
FAR = (4, 5, 3, 6, 2, 7, 1)
NEAR = FAR[::-1]


def kernel(
    res_hbm, q_hbm, k_hbm, v_hbm, gain_hbm, wg_hbm, wu_hbm, wd_hbm,
    pt_hbm, lens_hbm, ids_hbm, gates_hbm,
    out_ref,
    pt, lens, ids, gates, res, q, kp, vp, gain, wgu, wt, wd,
    s24, blk, p1, f16, xall, pay, rsb, hid, r1s, r1r, r2s, r2r,
    ld_sem, p1_s, p1_r, p2_s, p2_r, rs_s, rs_r, ag_s, ag_r,
    wx_s, wx_r, r1_s, r1_r, r2_sm, r2_rm,
):
    sec, grp, x = lax.axis_index("sec"), lax.axis_index("grp"), lax.axis_index("tp")
    y, z, c = sec * 4 + grp // 16, (grp // 2) % 8, grp % 2

    def dev(yy, zz, cc, xx):
        return (yy // 4, (yy % 4) * 16 + zz * 2 + cc, xx)

    def first(k):
        return dev((y + k * (1 - c)) % RING, (z + k * c) % RING, c, x)

    def second(k):
        return dev((y + k * c) % RING, (z + k * (1 - c)) % RING, c, x)

    def along(e):
        return dev(y, z, c, (x + e) % NX)

    other = dev(y, z, 1 - c, x)

    barrier = pltpu.get_barrier_semaphore()
    peers = [ring(k) for k in FAR for ring in (first, second)]
    peers += [along(e) for e in range(1, NX)] + [other]
    for peer in peers:
        pl.semaphore_signal(barrier, inc=1, device_id=peer, device_id_type=MESH)

    loads = []
    for i, (a, b) in enumerate((
        (pt_hbm, pt), (lens_hbm, lens), (ids_hbm, ids), (gates_hbm, gates),
        (q_hbm, q), (k_hbm, kp), (v_hbm, vp), (res_hbm, res), (gain_hbm, gain),
        (wg_hbm, wgu.at[pl.ds(0, FFD)]), (wu_hbm, wgu.at[pl.ds(FFP, FFD)]),
        (wd_hbm, wd.at[pl.ds(0, FFD)]),
    )):
        cp = pltpu.make_async_copy(a, b, ld_sem.at[i])
        cp.start()
        loads.append(cp)

    pending = []

    def send(src, dst, ssem, rsem, to):
        cp = pltpu.make_async_remote_copy(
            src_ref=src, dst_ref=dst, send_sem=ssem, recv_sem=rsem,
            device_id=to, device_id_type=MESH,
        )
        cp.start()
        pending.append(cp)
        return cp

    lane = lax.broadcasted_iota(jnp.int32, (8, KV), 1)
    row = lax.broadcasted_iota(jnp.int32, (8, KV), 0)
    page = lane // PAGE
    slot = jnp.zeros((8, KV), jnp.int32)
    loads[0].wait()
    loads[1].wait()
    for j in range(PAGES):
        slot = jnp.where(page == pt[0, j], j, slot)
    late = slot >= PAGES // 2
    pos = (slot - jnp.where(late, PAGES // 2, 0)) * PAGE + lane % PAGE
    visible = (pos < jnp.where(late, lens[0, 1], lens[0, 0])) & (
        jnp.where(late, 1, 0) == row % 2
    )
    hidden_tokens = jnp.where(visible, 0.0, F32(-1e30))
    hidden_tokens = jnp.concatenate([hidden_tokens] * 3, axis=0)
    loads[2].wait()
    loads[3].wait()
    lane8 = lax.broadcasted_iota(jnp.int32, (8, HD), 1)
    row8 = lax.broadcasted_iota(jnp.int32, (8, HD), 0)
    weight = jnp.zeros((8, HD), F32)
    total = jnp.ones((8, HD), F32)
    for s in range(2):
        here = row8 == s
        total = jnp.where(
            here, gates[s, 0] + gates[s, 1] + gates[s, 2] + gates[s, 3], total
        )
        for k in range(4):
            hit = here & (lane8 < 16) & (lane8 % 8 == ids[s, k])
            weight = jnp.where(hit, gates[s, k], weight)
    weight = weight / total

    for top in (FFD, FFP + FFD):
        wd[top : top + FFP - FFD, :] = jnp.zeros((FFP - FFD, COLS), BF16)
    for top in (FFD, FFP + FFD):
        wgu[top : top + FFP - FFD, :] = jnp.zeros((FFP - FFD, COLS), BF16)

    def stack(value):
        for h in range(HEADS_DEV):
            s24[2 * h : 2 * h + 2, :] = value[:, h * HD : (h + 1) * HD]
        return s24[...]

    nt = (((1,), (1,)), ((), ()))
    loads[4].wait()
    q24 = stack(q[...].astype(F32)).astype(BF16)
    loads[5].wait()
    keys = kp[...].reshape(KV, 2 * HD)
    head0 = lax.broadcasted_iota(jnp.int32, (24, KV), 0) < 12
    scores = jnp.where(
        head0,
        lax.dot_general(q24, keys[:, :HD], nt, preferred_element_type=F32),
        lax.dot_general(q24, keys[:, HD:], nt, preferred_element_type=F32),
    ) * (HD ** -0.5)
    scores = jnp.where(hidden_tokens < 0.0, hidden_tokens, scores)
    expo = jnp.exp(scores - jnp.max(scores, axis=1, keepdims=True))
    probs = (expo / jnp.sum(expo, axis=1, keepdims=True)).astype(BF16)
    loads[6].wait()
    values = vp[...].reshape(KV, 2 * HD)
    attn = jnp.dot(probs, values, preferred_element_type=F32)
    row24 = lax.broadcasted_iota(jnp.int32, (24, HD), 0)
    attn = jnp.where(row24 < 12, attn[:, :HD], attn[:, HD:])
    loads[7].wait()
    stream = (stack(res[...].astype(F32)) + attn).astype(BF16).astype(F32)
    loads[8].wait()
    gains = gain[...].astype(F32).reshape(HEADS_DEV, HD)
    for h in range(HEADS_DEV):
        s24[2 * h : 2 * h + 2, :] = jnp.broadcast_to(gains[h : h + 1, :], (2, HD))
    gain24 = s24[...]
    square = jnp.sum(stream * stream, axis=1, keepdims=True)
    odd = lax.broadcasted_iota(jnp.int32, (24, 1), 0) % 2 == 1
    ss0 = jnp.sum(jnp.where(odd, 0.0, square), axis=0, keepdims=True)
    ss1 = jnp.sum(jnp.where(odd, square, 0.0), axis=0, keepdims=True)
    ss = jnp.where(row8 == 0, ss0, ss1)
    w_hi = weight.astype(BF16).astype(F32)
    ss_hi = ss.astype(BF16).astype(F32)
    extra = jnp.where(lane8 < 8, w_hi, jnp.where(lane8 < 16, weight - w_hi, 0.0))
    extra = jnp.where(lane8 == SS_HI, ss_hi, extra)
    extra = jnp.where(lane8 == SS_LO, ss - ss_hi, extra)
    extra = jnp.where(row8 < 2, extra, 0.0)
    blk[...] = jnp.concatenate([stream * gain24, extra], axis=0).astype(BF16)

    pl.semaphore_wait(barrier, len(peers))

    arrive1 = [
        send(blk, p1.at[k], p1_s.at[k], p1_r.at[k], first(k)) for k in range(1, RING)
    ]

    for cp in loads[9:]:
        cp.wait()
    for part in range(2):
        for t in range(0, FFP, HD):
            left = part * WIDE + t
            wt[:, left : left + HD] = wgu[part * FFP + t : part * FFP + t + HD, :].T
    weights = [
        send(src, dst, wx_s.at[i], wx_r.at[i], other)
        for i, (src, dst) in enumerate((
            (wt.at[:, pl.ds(0, FFP)], wt.at[:, pl.ds(FFP, FFP)]),
            (wt.at[:, pl.ds(WIDE, FFP)], wt.at[:, pl.ds(WIDE + FFP, FFP)]),
            (wd.at[pl.ds(0, FFD)], wd.at[pl.ds(FFP, FFD)]),
        ))
    ]

    def place(k, value):
        for t in range(EXT // HD):
            f16[2 * k : 2 * k + 2, t * HD : (t + 1) * HD] = value[2 * t : 2 * t + 2, :]

    place(0, blk[...].astype(F32))
    for k in NEAR:
        arrive1[k - 1].wait_recv()
        place(k, p1[k].astype(F32))
    own = pl.ds(ROW[0], 16)
    xall[own, :] = f16[...].astype(BF16)

    arrive2 = {
        m: send(
            xall.at[own], xall.at[pl.ds(ROW[m], 16)], p2_s.at[m], p2_r.at[m], second(m)
        )
        for m in FAR
    }

    rs, ag, back = {}, {}, {}

    def quarter(j, q):
        size = 4 * len(CHUNKS[j])
        return pl.ds(pl.multiple_of(16 * BASE[j] + q * size, 16), size)

    def gate_up(j):
        n = len(CHUNKS[j])
        for m in CHUNKS[j]:
            if m:
                arrive2[m].wait_recv()
        if j == 0:
            weights[0].wait_recv()
            weights[1].wait_recv()
        rows = pl.ds(16 * BASE[j], 16 * n)
        both = jnp.dot(xall[rows, 0:COLS], wt[...], preferred_element_type=F32)
        lane = lax.broadcasted_iota(jnp.int32, (16 * n, HD), 1)
        extras = xall[rows, COLS:EXT].astype(F32)
        tile = jnp.where(lane >= FFD % HD, extras, both[:, 256:FFP])
        pay[rows, 0:256] = both[:, 0:256].astype(BF16)
        pay[rows, 256:FFP] = tile.astype(BF16)
        pay[rows, FFP:] = both[:, FFP:].astype(BF16)
        piece = pl.ds(4 * BASE[j], 4 * n)
        rs[j] = [
            send(
                pay.at[quarter(j, (x + e) % NX)], rsb.at[e, piece],
                rs_s.at[j, e], rs_r.at[j, e], along(e),
            )
            for e in (2, 1, 3)
        ]

    def activate(j):
        n = len(CHUNKS[j])
        both = pay[quarter(j, x), :].astype(F32)
        lane = lax.broadcasted_iota(jnp.int32, (4 * n, HD), 1)
        weight = jnp.sum(
            jnp.where(
                (lane == y) | (lane == y + 8),
                xall[quarter(j, x), COLS:EXT].astype(F32), 0.0,
            ),
            axis=1, keepdims=True,
        )
        for cp, e in zip(rs[j], (2, 1, 3)):
            cp.wait_recv()
            both = both + rsb[e, pl.ds(4 * BASE[j], 4 * n), :].astype(F32)
        square = jnp.sum(
            jnp.where((lane == SS_HI) | (lane == SS_LO), both[:, 256:FFP], 0.0),
            axis=1, keepdims=True,
        )
        scale = lax.rsqrt(square / D + 1e-05)
        gate = both[:, 0:WIDE] * scale
        up = both[:, WIDE:] * (scale * weight)
        value = gate / (1.0 + jnp.exp(-gate)) * up
        unit = lax.broadcasted_iota(jnp.int32, (4 * n, WIDE), 1) % FFP
        mine = quarter(j, x)
        hid[mine, :] = jnp.where(unit < FFD, value, 0.0).astype(BF16)
        ag[j] = [
            send(hid.at[mine], hid.at[mine], ag_s.at[j, e], ag_r.at[j, e], along(e))
            for e in (2, 1, 3)
        ]

    def down(j):
        n = len(CHUNKS[j])
        if j == 0:
            weights[2].wait_recv()
        for cp in ag[j]:
            cp.wait_recv()
        half = pl.ds(16 * BASE[j], 16 * n)
        r1s[half, :] = jnp.dot(
            hid[half, :], wd[...], preferred_element_type=F32
        ).astype(BF16)
        for m in FAR:
            if m in CHUNKS[j]:
                back[m] = send(
                    r1s.at[pl.ds(ROW[m], 16)], r1r.at[m],
                    r1_s.at[m], r1_r.at[m], second(RING - m),
                )

    stages = {"G": gate_up, "A": activate, "D": down}
    for step in STEPS:
        stages[step[0]](int(step[1:]))

    total = r1s[pl.ds(ROW[0], 16), :].astype(F32)
    for m in NEAR:
        back[m].wait_recv()
        total = total + r1r[m].astype(F32)
    f16[:, 0:COLS] = total

    home = {}
    for k in FAR + (0,):
        for h in range(HEADS_DEV):
            s24[2 * h : 2 * h + 2, :] = f16[2 * k : 2 * k + 2, h * HD : (h + 1) * HD]
        if k:
            r2s[k, 0:24, :] = s24[...].astype(BF16)
            r2s[k, 24:32, :] = jnp.zeros((8, HD), BF16)
            home[k] = send(
                r2s.at[k], r2r.at[k], r2_sm.at[k], r2_rm.at[k], first(RING - k)
            )
    mixture = s24[...]
    for cp in pending[: -len(FAR)]:
        cp.wait_send()
    for k in NEAR:
        home[k].wait_recv()
        mixture = mixture + r2r[k, 0:24, :].astype(F32)
    out_ref[...] = (stream + mixture).astype(BF16)
    for cp in pending[-len(FAR) :]:
        cp.wait_send()


def shards(
    residual, queries, key_pages, value_pages, page_table, lengths, norm_gain,
    expert_ids, route_gates, w_gate, w_up, w_down,
):
    any_ = pl.BlockSpec(memory_space=pl.ANY)
    dma = pltpu.SemaphoreType.DMA
    out = pl.pallas_call(
        kernel,
        out_shape=jax.ShapeDtypeStruct((24, HD), BF16),
        in_specs=[any_] * 12,
        out_specs=pl.BlockSpec(memory_space=pltpu.VMEM),
        scratch_shapes=[
            pltpu.SMEM((1, PAGES), jnp.int32), pltpu.SMEM((1, 2), jnp.int32),
            pltpu.SMEM((2, 4), jnp.int32), pltpu.SMEM((2, 4), F32),
            pltpu.VMEM((2, COLS), BF16), pltpu.VMEM((2, COLS), BF16),
            pltpu.VMEM((PAGES, PAGE, 2 * HD), BF16), pltpu.VMEM((PAGES, PAGE, 2 * HD), BF16),
            pltpu.VMEM((COLS,), BF16),
            pltpu.VMEM((WIDE, COLS), BF16), pltpu.VMEM((COLS, 2 * WIDE), BF16),
            pltpu.VMEM((WIDE, COLS), BF16),
            pltpu.VMEM((24, HD), F32), pltpu.VMEM((BLK, HD), BF16),
            pltpu.VMEM((RING, BLK, HD), BF16), pltpu.VMEM((16, EXT), F32),
            pltpu.VMEM((128, EXT), BF16), pltpu.VMEM((128, 2 * WIDE), BF16),
            pltpu.VMEM((NX, 32, 2 * WIDE), BF16),
            pltpu.VMEM((128, WIDE), BF16),
            pltpu.VMEM((128, COLS), BF16), pltpu.VMEM((RING, 16, COLS), BF16),
            pltpu.VMEM((RING, BLK, HD), BF16), pltpu.VMEM((RING, BLK, HD), BF16),
            dma((12,)), dma((RING,)), dma((RING,)), dma((RING,)), dma((RING,)),
            dma((NC, NX)), dma((NC, NX)), dma((NC, NX)), dma((NC, NX)),
            dma((3,)), dma((3,)), dma((RING,)), dma((RING,)), dma((RING,)), dma((RING,)),
        ],
        compiler_params=pltpu.CompilerParams(
            collective_id=0, has_side_effects=True, vmem_limit_bytes=60 * 2**20
        ),
        name="decode_layer",
    )(
        residual, queries, key_pages, value_pages, norm_gain,
        w_gate.T, w_up.T, w_down, page_table, lengths, expert_ids, route_gates,
    )
    return out.reshape(HEADS_DEV, 2, HD).transpose(1, 0, 2).reshape(2, COLS)


def solution(mesh):
    rows, wide = ("sec", "grp"), "tp"
    return jax.shard_map(
        shards,
        mesh=mesh,
        in_specs=(
            P(rows, wide), P(rows, wide), P(rows, None, wide), P(rows, None, wide),
            P(rows, None), P(rows, None), P(wide), P(rows, None), P(rows, None),
            P(wide, rows), P(wide, rows), P(rows, wide),
        ),
        out_specs=P(rows, wide),
        check_vma=False,
    )
```

```python
import functools

import jax
import jax.numpy as jnp
from jax import lax
from jax.experimental import pallas as pl
from jax.experimental.pallas import tpu as pltpu
from jax.sharding import PartitionSpec as P

MESH = pl.DeviceIdType.MESH
BF16, F32 = jnp.bfloat16, jnp.float32

D = 6144
RING = 8
NX = 4
HEADS_DEV = 12
HD = 128
COLS = 1536
EXT = COLS + HD
FFD = 336
FFP = 384
WIDE = 2 * FFP
PAGES = 24
PAGE = 16
KV = PAGES * PAGE
BLK = 32
SS_HI, SS_LO = FFD % HD, FFD % HD + 1

CHUNKS = ((4, 5, 3, 6), (7, 2, 1, 0))
STEPS = ("G0", "G1", "A0", "A1", "D0", "D1")
NC = len(CHUNKS)
BASE = [sum(len(c) for c in CHUNKS[:j]) for j in range(NC)]
ROW = {m: 16 * (BASE[j] + i) for j, c in enumerate(CHUNKS) for i, m in enumerate(c)}
FAR = (4, 5, 3, 6, 2, 7, 1)
NEAR = FAR[::-1]


def kernel(
    res_hbm, q_hbm, k_hbm, v_hbm, gain_hbm, wg_hbm, wu_hbm, wd_hbm,
    pt_hbm, lens_hbm, ids_hbm, gates_hbm,
    out_ref,
    pt, lens, ids, gates, res, q, kp, vp, gain, wgu, wt, wd,
    s24, blk, p1, f16, xall, pay, rsb, hid, r1s, r1r, r2s, r2r,
    ld_sem, p1_s, p1_r, p2_s, p2_r, rs_s, rs_r, ag_s, ag_r,
    wx_s, wx_r, r1_s, r1_r, r2_sm, r2_rm,
):
    sec, grp, x = lax.axis_index("sec"), lax.axis_index("grp"), lax.axis_index("tp")
    y, z, c = sec * 4 + grp // 16, (grp // 2) % 8, grp % 2

    def dev(yy, zz, cc, xx):
        return (yy // 4, (yy % 4) * 16 + zz * 2 + cc, xx)

    def first(k):
        return dev((y + k * (1 - c)) % RING, (z + k * c) % RING, c, x)

    def second(k):
        return dev((y + k * c) % RING, (z + k * (1 - c)) % RING, c, x)

    def along(e):
        return dev(y, z, c, (x + e) % NX)

    other = dev(y, z, 1 - c, x)

    barrier = pltpu.get_barrier_semaphore()
    peers = [ring(k) for k in FAR for ring in (first, second)]
    peers += [along(e) for e in range(1, NX)] + [other]
    for peer in peers:
        pl.semaphore_signal(barrier, inc=1, device_id=peer, device_id_type=MESH)

    loads = []

    def load(*pairs):
        for src, dst in pairs:
            cp = pltpu.make_async_copy(src, dst, ld_sem.at[len(loads)])
            cp.start()
            loads.append(cp)

    load(
        (pt_hbm, pt), (lens_hbm, lens), (ids_hbm, ids), (gates_hbm, gates),
        (q_hbm, q), (k_hbm, kp), (v_hbm, vp), (res_hbm, res), (gain_hbm, gain),
    )
    pending = []

    def send(src, dst, ssem, rsem, to):
        cp = pltpu.make_async_remote_copy(
            src_ref=src, dst_ref=dst, send_sem=ssem, recv_sem=rsem,
            device_id=to, device_id_type=MESH,
        )
        cp.start()
        pending.append(cp)
        return cp

    lane = lax.broadcasted_iota(jnp.int32, (8, KV), 1)
    row = lax.broadcasted_iota(jnp.int32, (8, KV), 0)
    page = lane // PAGE
    slot = jnp.zeros((8, KV), jnp.int32)
    loads[0].wait()
    loads[1].wait()
    for j in range(PAGES):
        slot = jnp.where(page == pt[0, j], j, slot)
    late = slot >= PAGES // 2
    pos = (slot - jnp.where(late, PAGES // 2, 0)) * PAGE + lane % PAGE
    visible = (pos < jnp.where(late, lens[0, 1], lens[0, 0])) & (
        jnp.where(late, 1, 0) == row % 2
    )
    hidden_tokens = jnp.where(visible, 0.0, F32(-1e30))
    hidden_tokens = jnp.concatenate([hidden_tokens] * 3, axis=0)
    loads[2].wait()
    loads[3].wait()
    lane8 = lax.broadcasted_iota(jnp.int32, (8, HD), 1)
    row8 = lax.broadcasted_iota(jnp.int32, (8, HD), 0)
    weight = jnp.zeros((8, HD), F32)
    total = jnp.ones((8, HD), F32)
    for s in range(2):
        here = row8 == s
        total = jnp.where(
            here, gates[s, 0] + gates[s, 1] + gates[s, 2] + gates[s, 3], total
        )
        for k in range(4):
            hit = here & (lane8 < 16) & (lane8 % 8 == ids[s, k])
            weight = jnp.where(hit, gates[s, k], weight)
    weight = weight / total

    for top in (FFD, FFP + FFD):
        wd[top : top + FFP - FFD, :] = jnp.zeros((FFP - FFD, COLS), BF16)
    for top in (FFD, FFP + FFD):
        wgu[top : top + FFP - FFD, :] = jnp.zeros((FFP - FFD, COLS), BF16)

    def stack(value):
        for h in range(HEADS_DEV):
            s24[2 * h : 2 * h + 2, :] = value[:, h * HD : (h + 1) * HD]
        return s24[...]

    nt = (((1,), (1,)), ((), ()))
    loads[4].wait()
    q24 = stack(q[...].astype(F32)).astype(BF16)
    loads[5].wait()
    keys = kp[...].reshape(KV, 2 * HD)
    head0 = lax.broadcasted_iota(jnp.int32, (24, KV), 0) < 12
    scores = jnp.where(
        head0,
        lax.dot_general(q24, keys[:, :HD], nt, preferred_element_type=F32),
        lax.dot_general(q24, keys[:, HD:], nt, preferred_element_type=F32),
    ) * (HD ** -0.5)
    scores = jnp.where(hidden_tokens < 0.0, hidden_tokens, scores)
    expo = jnp.exp(scores - jnp.max(scores, axis=1, keepdims=True))
    probs = (expo / jnp.sum(expo, axis=1, keepdims=True)).astype(BF16)
    loads[6].wait()
    values = vp[...].reshape(KV, 2 * HD)
    attn = jnp.dot(probs, values, preferred_element_type=F32)
    row24 = lax.broadcasted_iota(jnp.int32, (24, HD), 0)
    attn = jnp.where(row24 < 12, attn[:, :HD], attn[:, HD:])
    loads[7].wait()
    stream = (stack(res[...].astype(F32)) + attn).astype(BF16).astype(F32)
    loads[8].wait()
    gains = gain[...].astype(F32).reshape(HEADS_DEV, HD)
    for h in range(HEADS_DEV):
        s24[2 * h : 2 * h + 2, :] = jnp.broadcast_to(gains[h : h + 1, :], (2, HD))
    gain24 = s24[...]
    square = jnp.sum(stream * stream, axis=1, keepdims=True)
    odd = lax.broadcasted_iota(jnp.int32, (24, 1), 0) % 2 == 1
    ss0 = jnp.sum(jnp.where(odd, 0.0, square), axis=0, keepdims=True)
    ss1 = jnp.sum(jnp.where(odd, square, 0.0), axis=0, keepdims=True)
    ss = jnp.where(row8 == 0, ss0, ss1)
    w_hi = weight.astype(BF16).astype(F32)
    ss_hi = ss.astype(BF16).astype(F32)
    extra = jnp.where(lane8 < 8, w_hi, jnp.where(lane8 < 16, weight - w_hi, 0.0))
    extra = jnp.where(lane8 == SS_HI, ss_hi, extra)
    extra = jnp.where(lane8 == SS_LO, ss - ss_hi, extra)
    extra = jnp.where(row8 < 2, extra, 0.0)
    blk[...] = jnp.concatenate([stream * gain24, extra], axis=0).astype(BF16)

    pl.semaphore_wait(barrier, len(peers))
    load(
        (wg_hbm, wgu.at[pl.ds(0, FFD)]), (wu_hbm, wgu.at[pl.ds(FFP, FFD)]),
        (wd_hbm, wd.at[pl.ds(0, FFD)]),
    )

    arrive1 = [
        send(blk, p1.at[k], p1_s.at[k], p1_r.at[k], first(k)) for k in FAR
    ]

    for cp in loads[9:]:
        cp.wait()
    for part in range(2):
        for t in range(0, FFP, HD):
            left = part * WIDE + t
            wt[:, left : left + HD] = wgu[part * FFP + t : part * FFP + t + HD, :].T
    weights = [
        send(src, dst, wx_s.at[i], wx_r.at[i], other)
        for i, (src, dst) in enumerate((
            (wt.at[:, pl.ds(0, FFP)], wt.at[:, pl.ds(FFP, FFP)]),
            (wt.at[:, pl.ds(WIDE, FFP)], wt.at[:, pl.ds(WIDE + FFP, FFP)]),
            (wd.at[pl.ds(0, FFD)], wd.at[pl.ds(FFP, FFD)]),
        ))
    ]

    def place(k, value):
        for t in range(EXT // HD):
            f16[2 * k : 2 * k + 2, t * HD : (t + 1) * HD] = value[2 * t : 2 * t + 2, :]

    place(0, blk[...].astype(F32))
    for k in NEAR:
        arrive1[FAR.index(k)].wait_recv()
        place(k, p1[k].astype(F32))
    own = pl.ds(ROW[0], 16)
    xall[own, :] = f16[...].astype(BF16)

    arrive2 = {
        m: send(
            xall.at[own], xall.at[pl.ds(ROW[m], 16)], p2_s.at[m], p2_r.at[m], second(m)
        )
        for m in FAR
    }

    rs, ag, back = {}, {}, {}

    def quarter(j, q):
        size = 4 * len(CHUNKS[j])
        return pl.ds(pl.multiple_of(16 * BASE[j] + q * size, 16), size)

    def gate_up(j):
        n = len(CHUNKS[j])
        for m in CHUNKS[j]:
            if m:
                arrive2[m].wait_recv()
        if j == 0:
            weights[0].wait_recv()
            weights[1].wait_recv()
        rows = pl.ds(16 * BASE[j], 16 * n)
        lane = lax.broadcasted_iota(jnp.int32, (16 * n, HD), 1)
        extras = xall[rows, COLS:EXT].astype(F32)
        piece = pl.ds(4 * BASE[j], 4 * n)
        rs[j] = {}
        for h in range(2):
            cols = pl.ds(h * WIDE, WIDE)
            half = jnp.dot(xall[rows, 0:COLS], wt[:, cols], preferred_element_type=F32)
            pay[rows, cols] = half.astype(BF16)
            if h == 0:
                tile = jnp.where(lane >= FFD % HD, extras, half[:, 256:FFP])
                pay[rows, 256:FFP] = tile.astype(BF16)
            for e in (2, 1, 3):
                rs[j][e, h] = send(
                    pay.at[quarter(j, (x + e) % NX), cols], rsb.at[e, piece, cols],
                    rs_s.at[j, e, h], rs_r.at[j, e, h], along(e),
                )

    def activate(j):
        n = len(CHUNKS[j])
        both = pay[quarter(j, x), :].astype(F32)
        lane = lax.broadcasted_iota(jnp.int32, (4 * n, HD), 1)
        weight = jnp.sum(
            jnp.where(
                (lane == y) | (lane == y + 8),
                xall[quarter(j, x), COLS:EXT].astype(F32), 0.0,
            ),
            axis=1, keepdims=True,
        )
        for e in (2, 1, 3):
            rs[j][e, 0].wait_recv()
            rs[j][e, 1].wait_recv()
            both = both + rsb[e, pl.ds(4 * BASE[j], 4 * n), :].astype(F32)
        square = jnp.sum(
            jnp.where((lane == SS_HI) | (lane == SS_LO), both[:, 256:FFP], 0.0),
            axis=1, keepdims=True,
        )
        scale = lax.rsqrt(square / D + 1e-05)
        gate = both[:, 0:WIDE] * scale
        up = both[:, WIDE:] * (scale * weight)
        value = gate / (1.0 + jnp.exp(-gate)) * up
        unit = lax.broadcasted_iota(jnp.int32, (4 * n, WIDE), 1) % FFP
        mine = quarter(j, x)
        hid[mine, :] = jnp.where(unit < FFD, value, 0.0).astype(BF16)
        ag[j] = [
            send(hid.at[mine], hid.at[mine], ag_s.at[j, e], ag_r.at[j, e], along(e))
            for e in (2, 1, 3)
        ]

    def down(j):
        n = len(CHUNKS[j])
        if j == 0:
            weights[2].wait_recv()
        for cp in ag[j]:
            cp.wait_recv()
        half = pl.ds(16 * BASE[j], 16 * n)
        r1s[half, :] = jnp.dot(
            hid[half, :], wd[...], preferred_element_type=F32
        ).astype(BF16)
        for m in FAR:
            if m in CHUNKS[j]:
                back[m] = send(
                    r1s.at[pl.ds(ROW[m], 16)], r1r.at[m],
                    r1_s.at[m], r1_r.at[m], second(RING - m),
                )

    stages = {"G": gate_up, "A": activate, "D": down}
    for step in STEPS:
        stages[step[0]](int(step[1:]))

    total = r1s[pl.ds(ROW[0], 16), :].astype(F32)
    for m in NEAR:
        back[m].wait_recv()
        total = total + r1r[m].astype(F32)
    f16[:, 0:COLS] = total

    home = {}
    for k in FAR + (0,):
        for h in range(HEADS_DEV):
            s24[2 * h : 2 * h + 2, :] = f16[2 * k : 2 * k + 2, h * HD : (h + 1) * HD]
        if k:
            r2s[k, 0:24, :] = s24[...].astype(BF16)
            r2s[k, 24:32, :] = jnp.zeros((8, HD), BF16)
            home[k] = send(
                r2s.at[k], r2r.at[k], r2_sm.at[k], r2_rm.at[k], first(RING - k)
            )
    mixture = s24[...]
    for cp in pending[: -len(FAR)]:
        cp.wait_send()
    for k in NEAR:
        home[k].wait_recv()
        mixture = mixture + r2r[k, 0:24, :].astype(F32)
    out_ref[...] = (stream + mixture).astype(BF16)
    for cp in pending[-len(FAR) :]:
        cp.wait_send()


def shards(
    residual, queries, key_pages, value_pages, page_table, lengths, norm_gain,
    expert_ids, route_gates, w_gate, w_up, w_down,
):
    any_ = pl.BlockSpec(memory_space=pl.ANY)
    dma = pltpu.SemaphoreType.DMA
    out = pl.pallas_call(
        kernel,
        out_shape=jax.ShapeDtypeStruct((24, HD), BF16),
        in_specs=[any_] * 12,
        out_specs=pl.BlockSpec(memory_space=pltpu.VMEM),
        scratch_shapes=[
            pltpu.SMEM((1, PAGES), jnp.int32), pltpu.SMEM((1, 2), jnp.int32),
            pltpu.SMEM((2, 4), jnp.int32), pltpu.SMEM((2, 4), F32),
            pltpu.VMEM((2, COLS), BF16), pltpu.VMEM((2, COLS), BF16),
            pltpu.VMEM((PAGES, PAGE, 2 * HD), BF16), pltpu.VMEM((PAGES, PAGE, 2 * HD), BF16),
            pltpu.VMEM((COLS,), BF16),
            pltpu.VMEM((WIDE, COLS), BF16), pltpu.VMEM((COLS, 2 * WIDE), BF16),
            pltpu.VMEM((WIDE, COLS), BF16),
            pltpu.VMEM((24, HD), F32), pltpu.VMEM((BLK, HD), BF16),
            pltpu.VMEM((RING, BLK, HD), BF16), pltpu.VMEM((16, EXT), F32),
            pltpu.VMEM((128, EXT), BF16), pltpu.VMEM((128, 2 * WIDE), BF16),
            pltpu.VMEM((NX, 32, 2 * WIDE), BF16),
            pltpu.VMEM((128, WIDE), BF16),
            pltpu.VMEM((128, COLS), BF16), pltpu.VMEM((RING, 16, COLS), BF16),
            pltpu.VMEM((RING, BLK, HD), BF16), pltpu.VMEM((RING, BLK, HD), BF16),
            dma((12,)), dma((RING,)), dma((RING,)), dma((RING,)), dma((RING,)),
            dma((NC, NX, 2)), dma((NC, NX, 2)), dma((NC, NX)), dma((NC, NX)),
            dma((3,)), dma((3,)), dma((RING,)), dma((RING,)), dma((RING,)), dma((RING,)),
        ],
        compiler_params=pltpu.CompilerParams(
            collective_id=0, has_side_effects=True, vmem_limit_bytes=60 * 2**20
        ),
        name="decode_layer",
    )(
        residual, queries, key_pages, value_pages, norm_gain,
        w_gate.T, w_up.T, w_down, page_table, lengths, expert_ids, route_gates,
    )
    return out.reshape(HEADS_DEV, 2, HD).transpose(1, 0, 2).reshape(2, COLS)


def solution(mesh):
    rows, wide = ("sec", "grp"), "tp"
    return jax.shard_map(
        shards,
        mesh=mesh,
        in_specs=(
            P(rows, wide), P(rows, wide), P(rows, None, wide), P(rows, None, wide),
            P(rows, None), P(rows, None), P(wide), P(rows, None), P(rows, None),
            P(wide, rows), P(wide, rows), P(rows, wide),
        ),
        out_specs=P(rows, wide),
        check_vma=False,
    )
```

```python
import functools

import jax
import jax.numpy as jnp
from jax import lax
from jax.experimental import pallas as pl
from jax.experimental.pallas import tpu as pltpu
from jax.sharding import PartitionSpec as P

MESH = pl.DeviceIdType.MESH
BF16, F32 = jnp.bfloat16, jnp.float32

D = 6144
RING = 8
NX = 4
HEADS_DEV = 12
HD = 128
COLS = 1536
EXT = COLS + HD
FFD = 336
FFP = 384
WIDE = 2 * FFP
PAGES = 24
PAGE = 16
KV = PAGES * PAGE
BLK = 32
SS_HI, SS_LO = FFD % HD, FFD % HD + 1

CHUNKS = ((4, 5, 3, 6), (7, 2, 1, 0))
STEPS = ("G0", "G1", "A0", "A1", "D0", "D1")
NC = len(CHUNKS)
BASE = [sum(len(c) for c in CHUNKS[:j]) for j in range(NC)]
ROW = {m: 16 * (BASE[j] + i) for j, c in enumerate(CHUNKS) for i, m in enumerate(c)}
FAR = (4, 5, 3, 6, 2, 7, 1)
NEAR = FAR[::-1]


def kernel(
    res_hbm, q_hbm, k_hbm, v_hbm, gain_hbm, wg_hbm, wu_hbm, wd_hbm,
    pt_hbm, lens_hbm, ids_hbm, gates_hbm,
    out_ref,
    pt, lens, ids, gates, res, q, kp, vp, gain, wgu, wt, wd,
    s24, blk, p1, f16, xall, pay, rsb, hid, r1s, r1r, r2s, r2r,
    ld_sem, p1_s, p1_r, p2_s, p2_r, rs_s, rs_r, ag_s, ag_r,
    wx_s, wx_r, r1_s, r1_r, r2_sm, r2_rm,
):
    sec, grp, x = lax.axis_index("sec"), lax.axis_index("grp"), lax.axis_index("tp")
    y, z, c = sec * 4 + grp // 16, (grp // 2) % 8, grp % 2

    def dev(yy, zz, cc, xx):
        return (yy // 4, (yy % 4) * 16 + zz * 2 + cc, xx)

    def first(k):
        return dev((y + k * (1 - c)) % RING, (z + k * c) % RING, c, x)

    def second(k):
        return dev((y + k * c) % RING, (z + k * (1 - c)) % RING, c, x)

    def along(e):
        return dev(y, z, c, (x + e) % NX)

    other = dev(y, z, 1 - c, x)

    barrier = pltpu.get_barrier_semaphore()
    peers = [ring(k) for k in FAR for ring in (first, second)]
    peers += [along(e) for e in range(1, NX)] + [other]
    for peer in peers:
        pl.semaphore_signal(barrier, inc=1, device_id=peer, device_id_type=MESH)

    loads = []

    def load(*pairs):
        for src, dst in pairs:
            cp = pltpu.make_async_copy(src, dst, ld_sem.at[len(loads)])
            cp.start()
            loads.append(cp)

    load(
        (pt_hbm, pt), (lens_hbm, lens), (ids_hbm, ids), (gates_hbm, gates),
        (q_hbm, q), (k_hbm, kp), (v_hbm, vp), (res_hbm, res), (gain_hbm, gain),
    )
    pending = []

    def send(src, dst, ssem, rsem, to):
        cp = pltpu.make_async_remote_copy(
            src_ref=src, dst_ref=dst, send_sem=ssem, recv_sem=rsem,
            device_id=to, device_id_type=MESH,
        )
        cp.start()
        pending.append(cp)
        return cp

    lane = lax.broadcasted_iota(jnp.int32, (8, KV), 1)
    row = lax.broadcasted_iota(jnp.int32, (8, KV), 0)
    page = lane // PAGE
    slot = jnp.zeros((8, KV), jnp.int32)
    loads[0].wait()
    loads[1].wait()
    for j in range(PAGES):
        slot = jnp.where(page == pt[0, j], j, slot)
    late = slot >= PAGES // 2
    pos = (slot - jnp.where(late, PAGES // 2, 0)) * PAGE + lane % PAGE
    visible = (pos < jnp.where(late, lens[0, 1], lens[0, 0])) & (
        jnp.where(late, 1, 0) == row % 2
    )
    hidden_tokens = jnp.where(visible, 0.0, F32(-1e30))
    hidden_tokens = jnp.concatenate([hidden_tokens] * 3, axis=0)
    loads[2].wait()
    loads[3].wait()
    lane8 = lax.broadcasted_iota(jnp.int32, (8, HD), 1)
    row8 = lax.broadcasted_iota(jnp.int32, (8, HD), 0)
    weight = jnp.zeros((8, HD), F32)
    total = jnp.ones((8, HD), F32)
    for s in range(2):
        here = row8 == s
        total = jnp.where(
            here, gates[s, 0] + gates[s, 1] + gates[s, 2] + gates[s, 3], total
        )
        for k in range(4):
            hit = here & (lane8 < 16) & (lane8 % 8 == ids[s, k])
            weight = jnp.where(hit, gates[s, k], weight)
    weight = weight / total

    for top in (FFD, FFP + FFD):
        wd[top : top + FFP - FFD, :] = jnp.zeros((FFP - FFD, COLS), BF16)
    for top in (FFD, FFP + FFD):
        wgu[top : top + FFP - FFD, :] = jnp.zeros((FFP - FFD, COLS), BF16)

    def stack(value):
        for h in range(HEADS_DEV):
            s24[2 * h : 2 * h + 2, :] = value[:, h * HD : (h + 1) * HD]
        return s24[...]

    nt = (((1,), (1,)), ((), ()))
    loads[4].wait()
    q24 = stack(q[...].astype(F32)).astype(BF16)
    loads[5].wait()
    keys = kp[...].reshape(KV, 2 * HD)
    head0 = lax.broadcasted_iota(jnp.int32, (24, KV), 0) < 12
    scores = jnp.where(
        head0,
        lax.dot_general(q24, keys[:, :HD], nt, preferred_element_type=F32),
        lax.dot_general(q24, keys[:, HD:], nt, preferred_element_type=F32),
    ) * (HD ** -0.5)
    scores = jnp.where(hidden_tokens < 0.0, hidden_tokens, scores)
    expo = jnp.exp(scores - jnp.max(scores, axis=1, keepdims=True))
    probs = (expo / jnp.sum(expo, axis=1, keepdims=True)).astype(BF16)
    loads[6].wait()
    values = vp[...].reshape(KV, 2 * HD)
    attn = jnp.dot(probs, values, preferred_element_type=F32)
    row24 = lax.broadcasted_iota(jnp.int32, (24, HD), 0)
    attn = jnp.where(row24 < 12, attn[:, :HD], attn[:, HD:])
    loads[7].wait()
    stream = (stack(res[...].astype(F32)) + attn).astype(BF16).astype(F32)
    loads[8].wait()
    gains = gain[...].astype(F32).reshape(HEADS_DEV, HD)
    for h in range(HEADS_DEV):
        s24[2 * h : 2 * h + 2, :] = jnp.broadcast_to(gains[h : h + 1, :], (2, HD))
    gain24 = s24[...]
    square = jnp.sum(stream * stream, axis=1, keepdims=True)
    odd = lax.broadcasted_iota(jnp.int32, (24, 1), 0) % 2 == 1
    ss0 = jnp.sum(jnp.where(odd, 0.0, square), axis=0, keepdims=True)
    ss1 = jnp.sum(jnp.where(odd, square, 0.0), axis=0, keepdims=True)
    ss = jnp.where(row8 == 0, ss0, ss1)
    w_hi = weight.astype(BF16).astype(F32)
    ss_hi = ss.astype(BF16).astype(F32)
    extra = jnp.where(lane8 < 8, w_hi, jnp.where(lane8 < 16, weight - w_hi, 0.0))
    extra = jnp.where(lane8 == SS_HI, ss_hi, extra)
    extra = jnp.where(lane8 == SS_LO, ss - ss_hi, extra)
    extra = jnp.where(row8 < 2, extra, 0.0)
    blk[...] = jnp.concatenate([stream * gain24, extra], axis=0).astype(BF16)

    pl.semaphore_wait(barrier, len(peers))
    load(
        (wg_hbm, wgu.at[pl.ds(0, FFD)]), (wu_hbm, wgu.at[pl.ds(FFP, FFD)]),
        (wd_hbm, wd.at[pl.ds(0, FFD)]),
    )

    arrive1 = [
        send(blk, p1.at[k], p1_s.at[k], p1_r.at[k], first(k)) for k in FAR
    ]

    for cp in loads[9:]:
        cp.wait()
    for part in range(2):
        for t in range(0, FFP, HD):
            left = part * WIDE + t
            wt[:, left : left + HD] = wgu[part * FFP + t : part * FFP + t + HD, :].T
    weights = [
        send(src, dst, wx_s.at[i], wx_r.at[i], other)
        for i, (src, dst) in enumerate((
            (wt.at[:, pl.ds(0, FFP)], wt.at[:, pl.ds(FFP, FFP)]),
            (wt.at[:, pl.ds(WIDE, FFP)], wt.at[:, pl.ds(WIDE + FFP, FFP)]),
            (wd.at[pl.ds(0, FFD)], wd.at[pl.ds(FFP, FFD)]),
        ))
    ]

    def place(k, value):
        for t in range(EXT // HD):
            f16[2 * k : 2 * k + 2, t * HD : (t + 1) * HD] = value[2 * t : 2 * t + 2, :]

    place(0, blk[...].astype(F32))
    for k in NEAR:
        arrive1[FAR.index(k)].wait_recv()
        place(k, p1[k].astype(F32))
    own = pl.ds(ROW[0], 16)
    xall[own, :] = f16[...].astype(BF16)

    arrive2 = {
        m: send(
            xall.at[own, pl.ds(0, COLS)], xall.at[pl.ds(ROW[m], 16), pl.ds(0, COLS)],
            p2_s.at[m, 0], p2_r.at[m, 0], second(m),
        )
        for m in FAR
    }
    last = pl.ds(COLS, HD)
    tails = {
        m: send(
            xall.at[own, last], xall.at[pl.ds(ROW[m], 16), last],
            p2_s.at[m, 1], p2_r.at[m, 1], second(m),
        )
        for m in FAR
    }

    rs, ag, back = {}, {}, {}

    def quarter(j, q):
        size = 4 * len(CHUNKS[j])
        return pl.ds(pl.multiple_of(16 * BASE[j] + q * size, 16), size)

    def gate_up(j):
        n = len(CHUNKS[j])
        for m in CHUNKS[j]:
            if m:
                arrive2[m].wait_recv()
        if j == 0:
            weights[0].wait_recv()
            weights[1].wait_recv()
        rows = pl.ds(16 * BASE[j], 16 * n)
        lane = lax.broadcasted_iota(jnp.int32, (16 * n, HD), 1)
        piece = pl.ds(4 * BASE[j], 4 * n)
        rs[j] = {}
        for h in range(2):
            cols = pl.ds(h * WIDE, WIDE)
            half = jnp.dot(xall[rows, 0:COLS], wt[:, cols], preferred_element_type=F32)
            pay[rows, cols] = half.astype(BF16)
            if h == 0:
                for m in CHUNKS[j]:
                    if m:
                        tails[m].wait_recv()
                extras = xall[rows, COLS:EXT].astype(F32)
                tile = jnp.where(lane >= FFD % HD, extras, half[:, 256:FFP])
                pay[rows, 256:FFP] = tile.astype(BF16)
            for e in (2, 1, 3):
                rs[j][e, h] = send(
                    pay.at[quarter(j, (x + e) % NX), cols], rsb.at[e, piece, cols],
                    rs_s.at[j, e, h], rs_r.at[j, e, h], along(e),
                )

    def activate(j):
        n = len(CHUNKS[j])
        both = pay[quarter(j, x), :].astype(F32)
        lane = lax.broadcasted_iota(jnp.int32, (4 * n, HD), 1)
        weight = jnp.sum(
            jnp.where(
                (lane == y) | (lane == y + 8),
                xall[quarter(j, x), COLS:EXT].astype(F32), 0.0,
            ),
            axis=1, keepdims=True,
        )
        for e in (2, 1, 3):
            rs[j][e, 0].wait_recv()
            rs[j][e, 1].wait_recv()
            both = both + rsb[e, pl.ds(4 * BASE[j], 4 * n), :].astype(F32)
        square = jnp.sum(
            jnp.where((lane == SS_HI) | (lane == SS_LO), both[:, 256:FFP], 0.0),
            axis=1, keepdims=True,
        )
        scale = lax.rsqrt(square / D + 1e-05)
        gate = both[:, 0:WIDE] * scale
        up = both[:, WIDE:] * (scale * weight)
        value = gate / (1.0 + jnp.exp(-gate)) * up
        unit = lax.broadcasted_iota(jnp.int32, (4 * n, WIDE), 1) % FFP
        mine = quarter(j, x)
        hid[mine, :] = jnp.where(unit < FFD, value, 0.0).astype(BF16)
        ag[j] = [
            send(hid.at[mine], hid.at[mine], ag_s.at[j, e], ag_r.at[j, e], along(e))
            for e in (2, 1, 3)
        ]

    def down(j):
        n = len(CHUNKS[j])
        if j == 0:
            weights[2].wait_recv()
        for cp in ag[j]:
            cp.wait_recv()
        half = pl.ds(16 * BASE[j], 16 * n)
        r1s[half, :] = jnp.dot(
            hid[half, :], wd[...], preferred_element_type=F32
        ).astype(BF16)
        for m in FAR:
            if m in CHUNKS[j]:
                back[m] = send(
                    r1s.at[pl.ds(ROW[m], 16)], r1r.at[m],
                    r1_s.at[m], r1_r.at[m], second(RING - m),
                )

    stages = {"G": gate_up, "A": activate, "D": down}
    for step in STEPS:
        stages[step[0]](int(step[1:]))

    total = r1s[pl.ds(ROW[0], 16), :].astype(F32)
    for m in NEAR:
        back[m].wait_recv()
        total = total + r1r[m].astype(F32)
    f16[:, 0:COLS] = total

    home = {}
    for k in FAR + (0,):
        for h in range(HEADS_DEV):
            s24[2 * h : 2 * h + 2, :] = f16[2 * k : 2 * k + 2, h * HD : (h + 1) * HD]
        if k:
            r2s[k, 0:24, :] = s24[...].astype(BF16)
            r2s[k, 24:32, :] = jnp.zeros((8, HD), BF16)
            home[k] = send(
                r2s.at[k], r2r.at[k], r2_sm.at[k], r2_rm.at[k], first(RING - k)
            )
    mixture = s24[...]
    for cp in pending[: -len(FAR)]:
        cp.wait_send()
    for k in NEAR:
        home[k].wait_recv()
        mixture = mixture + r2r[k, 0:24, :].astype(F32)
    out_ref[...] = (stream + mixture).astype(BF16)
    for cp in pending[-len(FAR) :]:
        cp.wait_send()


def shards(
    residual, queries, key_pages, value_pages, page_table, lengths, norm_gain,
    expert_ids, route_gates, w_gate, w_up, w_down,
):
    any_ = pl.BlockSpec(memory_space=pl.ANY)
    dma = pltpu.SemaphoreType.DMA
    out = pl.pallas_call(
        kernel,
        out_shape=jax.ShapeDtypeStruct((24, HD), BF16),
        in_specs=[any_] * 12,
        out_specs=pl.BlockSpec(memory_space=pltpu.VMEM),
        scratch_shapes=[
            pltpu.SMEM((1, PAGES), jnp.int32), pltpu.SMEM((1, 2), jnp.int32),
            pltpu.SMEM((2, 4), jnp.int32), pltpu.SMEM((2, 4), F32),
            pltpu.VMEM((2, COLS), BF16), pltpu.VMEM((2, COLS), BF16),
            pltpu.VMEM((PAGES, PAGE, 2 * HD), BF16), pltpu.VMEM((PAGES, PAGE, 2 * HD), BF16),
            pltpu.VMEM((COLS,), BF16),
            pltpu.VMEM((WIDE, COLS), BF16), pltpu.VMEM((COLS, 2 * WIDE), BF16),
            pltpu.VMEM((WIDE, COLS), BF16),
            pltpu.VMEM((24, HD), F32), pltpu.VMEM((BLK, HD), BF16),
            pltpu.VMEM((RING, BLK, HD), BF16), pltpu.VMEM((16, EXT), F32),
            pltpu.VMEM((128, EXT), BF16), pltpu.VMEM((128, 2 * WIDE), BF16),
            pltpu.VMEM((NX, 32, 2 * WIDE), BF16),
            pltpu.VMEM((128, WIDE), BF16),
            pltpu.VMEM((128, COLS), BF16), pltpu.VMEM((RING, 16, COLS), BF16),
            pltpu.VMEM((RING, BLK, HD), BF16), pltpu.VMEM((RING, BLK, HD), BF16),
            dma((12,)), dma((RING,)), dma((RING,)), dma((RING, 2)), dma((RING, 2)),
            dma((NC, NX, 2)), dma((NC, NX, 2)), dma((NC, NX)), dma((NC, NX)),
            dma((3,)), dma((3,)), dma((RING,)), dma((RING,)), dma((RING,)), dma((RING,)),
        ],
        compiler_params=pltpu.CompilerParams(
            collective_id=0, has_side_effects=True, vmem_limit_bytes=60 * 2**20
        ),
        name="decode_layer",
    )(
        residual, queries, key_pages, value_pages, norm_gain,
        w_gate.T, w_up.T, w_down, page_table, lengths, expert_ids, route_gates,
    )
    return out.reshape(HEADS_DEV, 2, HD).transpose(1, 0, 2).reshape(2, COLS)


def solution(mesh):
    rows, wide = ("sec", "grp"), "tp"
    return jax.shard_map(
        shards,
        mesh=mesh,
        in_specs=(
            P(rows, wide), P(rows, wide), P(rows, None, wide), P(rows, None, wide),
            P(rows, None), P(rows, None), P(wide), P(rows, None), P(rows, None),
            P(wide, rows), P(wide, rows), P(rows, wide),
        ),
        out_specs=P(rows, wide),
        check_vma=False,
    )
```
